32 devices in a mesh: groups: 2 (over y), blk: 4 (over z), team: 2 (over x), head: 2 (over core).
Axes of the slice: x: 2, y: 2, z: 4, core: 2. Of those that a mesh axis runs over, the one named last changes fastest.
Arguments:
- queries: bfloat16 [768, 2560], P(('groups', 'blk', 'team'), 'head'), parts along dimension 0, may hold values from -8 to 8
- key_rows: bfloat16 [768, 2560], P(('groups', 'blk', 'team'), 'head'), parts along dimension 0, may hold values from -8 to 8
- value_rows: bfloat16 [768, 2560], P(('groups', 'blk', 'team'), 'head'), parts along dimension 0, may hold values from -6 to 6
Outputs:
- attended: bfloat16 [768, 2560], P(('groups', 'blk', 'team'), 'head'), parts along dimension 0
The draws below stay inside these ranges and needn't reach their ends.
There are 2 independent parts, one for each index of `groups`. The reference program is written for one: setup_inputs(seed, part) draws one part's arguments, and reference() takes and returns one part's arrays. A program takes and returns all parts, laid end to end along the dimension named above; each array names one. Nothing has to cross between parts.
All inputs are finite; a program needn't handle non-finite values.
Results may differ from the reference program's by a relative error of at most 0.009.
Values may be sent and summed in bfloat16 or wider, within the bound.
A program may use at most 64 MiB of HBM per device.

```python
import math
import jax
import jax.numpy as jnp
from jax import lax

HD = 128
H = 20
SEQ = 384


def rough_rows(base_key, salt_value):
    noise_key = jax.random.fold_in(base_key, salt_value)
    return jax.random.normal(noise_key, (SEQ, H * HD), jnp.float32)


def draw_queries(key, part):
    entries = rough_rows(key, 1)
    return jnp.clip(entries, -8.0, 8.0).astype(jnp.bfloat16)


def draw_key_rows(key, part):
    entries = rough_rows(key, 2)
    return jnp.clip(entries, -8.0, 8.0).astype(jnp.bfloat16)


def block_scale(own_key, dims, pieces, low, high):
    loudness, own = 1.0, jax.random.fold_in(own_key, 6)
    for dim, parts in pieces:
        draws = jnp.exp(jax.random.uniform(jax.random.fold_in(own, dim), (parts,), jnp.float32, low / len(pieces), high / len(pieces)))
        loudness = loudness * jnp.repeat(draws, dims[dim] // parts).reshape([-1 if axis == dim else 1 for axis in range(len(dims))])
    return loudness


def scatter_about(rng, extent, scale, bound, shards=(), dtype=jnp.bfloat16):
    result = scale * jax.random.normal(rng, extent, jnp.float32)
    if shards:
        result = result * block_scale(rng, extent, shards, -0.22, 0.18)
    return jnp.clip(result, -bound, bound).astype(dtype)


def setup_inputs(seed: int = 0, part: int = 0) -> dict:
    seeds = jax.random.split(jax.random.key(seed), 4)
    part_splits = jax.random.split(jax.random.fold_in(seeds[3], part), 4)
    return {
        "queries": draw_queries(jax.random.fold_in(jax.random.fold_in(seeds[3], part), 71), part),
        "key_rows": draw_key_rows(jax.random.fold_in(jax.random.fold_in(seeds[3], part), 71), part),
        "value_rows": scatter_about(part_splits[2], (SEQ, H * HD), 1.0, 6.0, ((0, 8), (1, 2))),
    }


def one_head(operands):
    query_head, key_head, value_head = operands
    scores = jnp.dot(query_head, key_head.T, preferred_element_type=jnp.float32) * (1.0 / math.sqrt(HD))
    row_top = lax.optimization_barrier(jnp.max(scores, axis=1, keepdims=True))
    weights = jnp.exp(scores - row_top)
    row_total = lax.optimization_barrier(jnp.sum(weights, axis=1, keepdims=True))
    mixed_head = jnp.dot(weights.astype(jnp.bfloat16), value_head, preferred_element_type=jnp.float32)
    return (mixed_head / row_total).astype(jnp.bfloat16)

def by_head(matrix):
    return matrix.reshape(SEQ, H, HD).transpose(1, 0, 2)

def reference(queries, key_rows, value_rows):
    attended = lax.map(one_head, (by_head(queries), by_head(key_rows), by_head(value_rows)))
    return attended.transpose(1, 0, 2).reshape(SEQ, H * HD)
```

```python
from functools import partial
import math

import jax
import jax.numpy as jnp
from jax import lax
from jax.experimental import pallas as pl
from jax.experimental.pallas import tpu as pltpu
from jax.sharding import PartitionSpec as P

HD = 128
MESH = pl.DeviceIdType.MESH


def attend_block(running, key_block, value_block, query_rows, score_scale):
    row_top, row_total, weighted = running
    scores = (
        jnp.einsum("qhd,khd->qhk", query_rows, key_block, preferred_element_type=jnp.float32)
        * score_scale
    )
    new_top = jnp.maximum(row_top, jnp.max(scores, axis=2))
    shrink = jnp.exp(row_top - new_top)
    weights = jnp.exp(scores - new_top[:, :, None])
    row_total = row_total * shrink + jnp.sum(weights, axis=2)
    weighted = weighted * shrink[:, :, None] + jnp.einsum(
        "qhk,khd->qhd",
        weights.astype(jnp.bfloat16),
        value_block,
        preferred_element_type=jnp.float32,
    )
    return (new_top, row_total, weighted)


def gathered(queries, key_rows, value_rows):
    own_rows = queries.shape[0]
    local_heads = queries.shape[1] // HD
    score_scale = 1.0 / math.sqrt(HD)
    query_heads = queries.reshape(own_rows, local_heads, HD)
    axes = ("blk", "team")
    keys = lax.all_gather(key_rows, axes, axis=0, tiled=True)
    values = lax.all_gather(value_rows, axes, axis=0, tiled=True)
    blocks = keys.shape[0] // own_rows
    keys = keys.reshape(blocks, own_rows, local_heads, HD)
    values = values.reshape(blocks, own_rows, local_heads, HD)

    def one_block(current, block_pair):
        return (attend_block(current, *block_pair, query_heads, score_scale), None)

    (_, row_total, weighted), _ = lax.scan(
        one_block,
        (
            jnp.full((own_rows, local_heads), -1e30, jnp.float32),
            jnp.zeros((own_rows, local_heads), jnp.float32),
            jnp.zeros((own_rows, local_heads, HD), jnp.float32),
        ),
        (keys, values),
    )
    mixed = weighted / row_total[:, :, None]
    return mixed.reshape(own_rows, local_heads * HD).astype(jnp.bfloat16)


def attend(q, k, v):
    scores = lax.dot_general(
        q, k, (((1,), (1,)), ((), ())), preferred_element_type=jnp.float32
    ) * (1.0 / math.sqrt(HD))
    top = jnp.max(scores, axis=1, keepdims=True)
    weights = jnp.exp(scores - top)
    total = jnp.sum(weights, axis=1, keepdims=True)
    mixed = jnp.dot(weights.astype(jnp.bfloat16), v, preferred_element_type=jnp.float32)
    return (mixed / total).astype(jnp.bfloat16)


def exchange_kernel(
    members, teams, whole, rest,
    q_ref, k_ref, v_ref, out_ref,
    qw, kw, vw, ow, qr, kr, vr, orest,
    send_sem, out_send_sem, recv_sem, rest_sem, out_sem,
):
    rows = q_ref.shape[0]
    me = lax.axis_index("blk") * teams + lax.axis_index("team")
    share = members // rest if rest else 0

    def where(member):
        return {"blk": member // teams, "team": member % teams}

    def at_rows(block):
        return pl.ds(pl.multiple_of(block * rows, rows), rows)

    def head_cols(head):
        return pl.ds(pl.multiple_of(head * HD, HD), HD)

    steps = sorted(range(1, members), key=lambda s: -min(s, members - s))
    others = [lax.rem(me + s, members) for s in steps]

    barrier = pltpu.get_barrier_semaphore()
    for other in others:
        pl.semaphore_signal(barrier, inc=1, device_id=where(other), device_id_type=MESH)
    for g in range(whole):
        for a, (src, dst) in enumerate(((k_ref, kw), (q_ref, qw), (v_ref, vw))):
            pltpu.make_async_copy(
                src.at[:, head_cols(me * whole + g)], dst.at[g, at_rows(me), :], recv_sem.at[a]
            ).start()
    if rest:
        mine = me // share
        for a, (src, dst) in enumerate(((k_ref, kr), (v_ref, vr))):
            pltpu.make_async_copy(
                src.at[:, head_cols(members * whole + mine)], dst.at[at_rows(me), :], rest_sem.at[a]
            ).start()
    pl.semaphore_wait(barrier, members - 1)

    sent = []

    def send(src, dst, sem, member):
        copy = pltpu.make_async_remote_copy(
            src_ref=src, dst_ref=dst, send_sem=send_sem, recv_sem=sem,
            device_id=where(member), device_id_type=MESH,
        )
        copy.start()
        sent.append(copy)

    for a, (src, dst) in enumerate(((k_ref, kw), (q_ref, qw), (v_ref, vw))):
        for other in others:
            for g in range(whole):
                send(
                    src.at[:, head_cols(other * whole + g)], dst.at[g, at_rows(me), :],
                    recv_sem.at[a], other,
                )
    if rest:
        part, slot = me // rest, me % rest
        for r in range(rest):
            owner = r * share + part
            src = q_ref.at[:, head_cols(members * whole + r)]
            dst = qr.at[at_rows(slot), :]

            @pl.when(owner == me)
            def _():
                pltpu.make_async_copy(src, dst, rest_sem.at[2]).start()

            @pl.when(owner != me)
            def _():
                pltpu.make_async_remote_copy(
                    src_ref=src, dst_ref=dst, send_sem=send_sem, recv_sem=rest_sem.at[2],
                    device_id=where(owner), device_id_type=MESH,
                ).start()
        for a, (src, dst) in enumerate(((k_ref, kr), (v_ref, vr))):
            for other in others:
                send(
                    src.at[:, head_cols(members * whole + other // share)], dst.at[at_rows(me), :],
                    rest_sem.at[a], other,
                )

    def arrived(ref, sem):
        pltpu.make_async_copy(ref, ref, sem).wait()

    def give(src, block, head):
        dst = out_ref.at[:, head_cols(head)]

        @pl.when(block == me)
        def _():
            pltpu.make_async_copy(src, dst, out_sem).start()

        @pl.when(block != me)
        def _():
            pltpu.make_async_remote_copy(
                src_ref=src, dst_ref=dst, send_sem=out_send_sem, recv_sem=out_sem,
                device_id=where(block), device_id_type=MESH,
            ).start()

    for a, ref in enumerate((kw, qw, vw)):
        arrived(ref, recv_sem.at[a])
    chunk = 2 if members % 2 == 0 else 1
    for g in range(whole):
        for c in range(0, members, chunk):
            span = pl.ds(c * rows, chunk * rows)
            ow[g, span, :] = attend(qw[g, span, :], kw[g], vw[g])
            for b in range(c, c + chunk):
                give(ow.at[g, pl.ds(b * rows, rows), :], jnp.int32(b), me * whole + g)
    if rest:
        for a, ref in enumerate((kr, vr, qr)):
            arrived(ref, rest_sem.at[a])
        orest[...] = attend(qr[...], kr[...], vr[...])
        for b in range(rest):
            give(
                orest.at[pl.ds(b * rows, rows), :], (me % share) * rest + b,
                members * whole + me // share,
            )

    for copy in sent:
        copy.wait_send()
    if rest:
        for r in range(rest):
            @pl.when(r * share + me // rest != me)
            def _():
                block = qr.at[pl.ds(0, rows), :]
                pltpu.make_async_copy(block, block, send_sem).wait()
    for b in range(members):
        @pl.when(b != me)
        def _():
            block = ow.at[:, pl.ds(0, rows), :]
            pltpu.make_async_copy(block, block, out_send_sem).wait()
    for b in range(rest):
        @pl.when((me % share) * rest + b != me)
        def _():
            block = orest.at[pl.ds(0, rows), :]
            pltpu.make_async_copy(block, block, out_send_sem).wait()
    arrived(out_ref, out_sem)


def exchanged(queries, key_rows, value_rows, *, teams, members, whole, rest):
    rows, columns = queries.shape
    bf16 = jnp.bfloat16
    full = pltpu.VMEM((whole, members * rows, HD), bf16)
    rest_full = pltpu.VMEM((members * rows, HD), bf16)
    rest_part = pltpu.VMEM((max(rest, 1) * rows, HD), bf16)
    return pl.pallas_call(
        partial(exchange_kernel, members, teams, whole, rest),
        out_shape=jax.ShapeDtypeStruct((rows, columns), bf16),
        in_specs=[pl.BlockSpec(memory_space=pl.ANY)] * 3,
        out_specs=pl.BlockSpec(memory_space=pl.ANY),
        scratch_shapes=[
            full, full, full, full, rest_part, rest_full, rest_full, rest_part,
            pltpu.SemaphoreType.DMA,
            pltpu.SemaphoreType.DMA,
            pltpu.SemaphoreType.DMA((3,)),
            pltpu.SemaphoreType.DMA((3,)),
            pltpu.SemaphoreType.DMA,
        ],
        compiler_params=pltpu.CompilerParams(collective_id=0, has_side_effects=True),
    )(queries, key_rows, value_rows)


def solution(mesh):
    teams, members = mesh.shape["team"], mesh.shape["blk"] * mesh.shape["team"]

    def local(queries, key_rows, value_rows):
        heads = queries.shape[1] // HD
        whole, rest = heads // members, heads % members
        if whole >= 1 and (rest == 0 or members % rest == 0):
            return exchanged(
                queries, key_rows, value_rows,
                teams=teams, members=members, whole=whole, rest=rest,
            )
        return gathered(queries, key_rows, value_rows)

    spec = P(("groups", "blk", "team"), "head")
    return jax.shard_map(
        local, mesh=mesh, in_specs=(spec,) * 3, out_specs=spec, check_vma=False
    )
```

```python
from functools import partial
import math

import jax
import jax.numpy as jnp
from jax import lax
from jax.experimental import pallas as pl
from jax.experimental.pallas import tpu as pltpu
from jax.sharding import PartitionSpec as P

HD = 128
MESH = pl.DeviceIdType.MESH


def attend_block(running, key_block, value_block, query_rows, score_scale):
    row_top, row_total, weighted = running
    scores = (
        jnp.einsum("qhd,khd->qhk", query_rows, key_block, preferred_element_type=jnp.float32)
        * score_scale
    )
    new_top = jnp.maximum(row_top, jnp.max(scores, axis=2))
    shrink = jnp.exp(row_top - new_top)
    weights = jnp.exp(scores - new_top[:, :, None])
    row_total = row_total * shrink + jnp.sum(weights, axis=2)
    weighted = weighted * shrink[:, :, None] + jnp.einsum(
        "qhk,khd->qhd",
        weights.astype(jnp.bfloat16),
        value_block,
        preferred_element_type=jnp.float32,
    )
    return (new_top, row_total, weighted)


def gathered(queries, key_rows, value_rows):
    own_rows = queries.shape[0]
    local_heads = queries.shape[1] // HD
    score_scale = 1.0 / math.sqrt(HD)
    query_heads = queries.reshape(own_rows, local_heads, HD)
    axes = ("blk", "team")
    keys = lax.all_gather(key_rows, axes, axis=0, tiled=True)
    values = lax.all_gather(value_rows, axes, axis=0, tiled=True)
    blocks = keys.shape[0] // own_rows
    keys = keys.reshape(blocks, own_rows, local_heads, HD)
    values = values.reshape(blocks, own_rows, local_heads, HD)

    def one_block(current, block_pair):
        return (attend_block(current, *block_pair, query_heads, score_scale), None)

    (_, row_total, weighted), _ = lax.scan(
        one_block,
        (
            jnp.full((own_rows, local_heads), -1e30, jnp.float32),
            jnp.zeros((own_rows, local_heads), jnp.float32),
            jnp.zeros((own_rows, local_heads, HD), jnp.float32),
        ),
        (keys, values),
    )
    mixed = weighted / row_total[:, :, None]
    return mixed.reshape(own_rows, local_heads * HD).astype(jnp.bfloat16)


def attend(q, k, v):
    scores = lax.dot_general(
        q, k, (((1,), (1,)), ((), ())), preferred_element_type=jnp.float32
    ) * (1.0 / math.sqrt(HD))
    top = jnp.max(scores, axis=1, keepdims=True)
    weights = jnp.exp(scores - top)
    total = jnp.sum(weights, axis=1, keepdims=True)
    mixed = jnp.dot(weights.astype(jnp.bfloat16), v, preferred_element_type=jnp.float32)
    return (mixed / total).astype(jnp.bfloat16)


def exchange_kernel(
    blks, teams, cores, whole, rest,
    q_ref, k_ref, v_ref, out_ref,
    qw, kw, vw, ow, qr, kvr, orest,
    send_sem, out_send_sem, recv_sem, direct_sem, passed_sem, rest_q_sem, out_sem,
):
    rows = q_ref.shape[0]
    members = blks * teams
    blk, team, core = lax.axis_index("blk"), lax.axis_index("team"), lax.axis_index("head")
    me = blk * teams + team

    def where(member, on_core=core):
        return {"blk": member // teams, "team": member % teams, "head": on_core}

    def at_rows(block):
        return pl.ds(pl.multiple_of(block * rows, rows), rows)

    def head_cols(head):
        return pl.ds(pl.multiple_of(head * HD, HD), HD)

    steps = sorted(range(1, members), key=lambda s: -min(s, members - s))
    others = [lax.rem(me + s, members) for s in steps]

    barrier = pltpu.get_barrier_semaphore()
    greeted = cores if rest else 1
    for turn in range(greeted):
        on_core = lax.rem(core + turn, cores)
        for other in others + ([me] if turn else []):
            pl.semaphore_signal(
                barrier, inc=1, device_id=where(other, on_core), device_id_type=MESH
            )
    for g in range(whole):
        for a, (src, dst) in enumerate(((k_ref, kw), (q_ref, qw), (v_ref, vw))):
            pltpu.make_async_copy(
                src.at[:, head_cols(me * whole + g)], dst.at[g, at_rows(me), :], recv_sem.at[a]
            ).start()
    pl.semaphore_wait(barrier, members * greeted - 1)

    def put(src, dst, here, device, sends, sem):
        @pl.when(here)
        def _():
            pltpu.make_async_copy(src, dst, sem).start()

        @pl.when(jnp.logical_not(here))
        def _():
            pltpu.make_async_remote_copy(
                src_ref=src, dst_ref=dst, send_sem=sends, recv_sem=sem,
                device_id=device, device_id_type=MESH,
            ).start()

    def arrived(ref, sem):
        pltpu.make_async_copy(ref, ref, sem).wait()

    part, slot = (me // rest, me % rest) if rest else (0, 0)
    for r in range(rest):
        home = core * rest + r
        cols = head_cols(members * whole + r)
        for a, src in enumerate((k_ref, v_ref)):
            put(
                src.at[:, cols], kvr.at[a, at_rows(me), :], home == blk,
                where(home * teams + team), send_sem, direct_sem.at[blk],
            )
        put(
            q_ref.at[:, cols], qr.at[at_rows(slot), :],
            (home == blk) & (part == team * cores + core),
            where(home * teams + part // cores, part % cores), send_sem, rest_q_sem,
        )
    sent = []
    for a, (src, dst) in enumerate(((k_ref, kw), (q_ref, qw), (v_ref, vw))):
        for other in others:
            for g in range(whole):
                copy = pltpu.make_async_remote_copy(
                    src_ref=src.at[:, head_cols(other * whole + g)],
                    dst_ref=dst.at[g, at_rows(me), :],
                    send_sem=send_sem, recv_sem=recv_sem.at[a],
                    device_id=where(other), device_id_type=MESH,
                )
                copy.start()
                sent.append(copy)

    if rest:
        @pl.when(blk // rest == core)
        def _():
            for b in range(blks):
                block = kvr.at[:, at_rows(b * teams + team), :]
                arrived(block, direct_sem.at[b])
                for turn in range(1, teams * cores):
                    t = lax.rem(team + turn // cores, teams)
                    pltpu.make_async_remote_copy(
                        src_ref=block, dst_ref=block, send_sem=send_sem, recv_sem=passed_sem,
                        device_id=where(blk * teams + t, lax.rem(core + turn % cores, cores)),
                        device_id_type=MESH,
                    ).start()

    for a, ref in enumerate((kw, qw, vw)):
        arrived(ref, recv_sem.at[a])
    chunk = 2 if members % 2 == 0 else 1
    for g in range(whole):
        for c in range(0, members, chunk):
            span = pl.ds(c * rows, chunk * rows)
            ow[g, span, :] = attend(qw[g, span, :], kw[g], vw[g])
            for b in range(c, c + chunk):
                put(
                    ow.at[g, pl.ds(b * rows, rows), :], out_ref.at[:, head_cols(me * whole + g)],
                    b == me, where(b), out_send_sem, out_sem,
                )
    first = (team * cores + core) * rest
    if rest:
        @pl.when(blk // rest == core)
        def _():
            if teams > 1:
                arrived(kvr.at[:, pl.ds(0, (teams - 1) * blks * rows), :], passed_sem)

        @pl.when(blk // rest != core)
        def _():
            arrived(kvr, passed_sem)

        arrived(qr, rest_q_sem)
        orest[...] = attend(qr[...], kvr[0], kvr[1])
        for b in range(rest):
            put(
                orest.at[pl.ds(b * rows, rows), :],
                out_ref.at[:, head_cols(members * whole + blk % rest)],
                (blk // rest == core) & (first + b == me),
                where(first + b, blk // rest), out_send_sem, out_sem,
            )

    for copy in sent:
        copy.wait_send()
    tile = ow.at[0, pl.ds(0, rows), :]
    for r in range(rest):
        home = core * rest + r

        @pl.when(home != blk)
        def _():
            for _ in range(2):
                arrived(tile, send_sem)

        @pl.when((home != blk) | (part != team * cores + core))
        def _():
            arrived(tile, send_sem)
    if rest:
        @pl.when(blk // rest == core)
        def _():
            for _ in range(teams * cores - 1):
                arrived(kvr.at[:, pl.ds(0, blks * rows), :], send_sem)
    for b in range(members):
        @pl.when(b != me)
        def _():
            arrived(ow.at[:, pl.ds(0, rows), :], out_send_sem)
    for b in range(rest):
        @pl.when((blk // rest != core) | (first + b != me))
        def _():
            arrived(tile, out_send_sem)
    arrived(out_ref, out_sem)


def exchanged(queries, key_rows, value_rows, *, blks, teams, cores, whole, rest):
    rows, columns = queries.shape
    members = blks * teams
    bf16 = jnp.bfloat16
    full = pltpu.VMEM((whole, members * rows, HD), bf16)
    rest_part = pltpu.VMEM((max(rest, 1) * rows, HD), bf16)
    return pl.pallas_call(
        partial(exchange_kernel, blks, teams, cores, whole, rest),
        out_shape=jax.ShapeDtypeStruct((rows, columns), bf16),
        in_specs=[pl.BlockSpec(memory_space=pl.ANY)] * 3,
        out_specs=pl.BlockSpec(memory_space=pl.ANY),
        scratch_shapes=[
            full, full, full, full,
            rest_part, pltpu.VMEM((2, members * rows, HD), bf16), rest_part,
            pltpu.SemaphoreType.DMA,
            pltpu.SemaphoreType.DMA,
            pltpu.SemaphoreType.DMA((3,)),
            pltpu.SemaphoreType.DMA((blks,)),
            pltpu.SemaphoreType.DMA,
            pltpu.SemaphoreType.DMA,
            pltpu.SemaphoreType.DMA,
        ],
        compiler_params=pltpu.CompilerParams(collective_id=0, has_side_effects=True),
    )(queries, key_rows, value_rows)


def solution(mesh):
    blks, teams, cores = (mesh.shape[name] for name in ("blk", "team", "head"))

    def local(queries, key_rows, value_rows):
        heads = queries.shape[1] // HD
        whole, rest = heads // (blks * teams), heads % (blks * teams)
        if whole >= 1 and rest * cores in (0, blks):
            return exchanged(
                queries, key_rows, value_rows,
                blks=blks, teams=teams, cores=cores, whole=whole, rest=rest,
            )
        return gathered(queries, key_rows, value_rows)

    spec = P(("groups", "blk", "team"), "head")
    return jax.shard_map(
        local, mesh=mesh, in_specs=(spec,) * 3, out_specs=spec, check_vma=False
    )
```

```python
from functools import partial
import math

import jax
import jax.numpy as jnp
from jax import lax
from jax.experimental import pallas as pl
from jax.experimental.pallas import tpu as pltpu
from jax.sharding import PartitionSpec as P

HD = 128
MESH = pl.DeviceIdType.MESH


def attend_block(running, key_block, value_block, query_rows, score_scale):
    row_top, row_total, weighted = running
    scores = (
        jnp.einsum("qhd,khd->qhk", query_rows, key_block, preferred_element_type=jnp.float32)
        * score_scale
    )
    new_top = jnp.maximum(row_top, jnp.max(scores, axis=2))
    shrink = jnp.exp(row_top - new_top)
    weights = jnp.exp(scores - new_top[:, :, None])
    row_total = row_total * shrink + jnp.sum(weights, axis=2)
    weighted = weighted * shrink[:, :, None] + jnp.einsum(
        "qhk,khd->qhd",
        weights.astype(jnp.bfloat16),
        value_block,
        preferred_element_type=jnp.float32,
    )
    return (new_top, row_total, weighted)


def gathered(queries, key_rows, value_rows):
    own_rows = queries.shape[0]
    local_heads = queries.shape[1] // HD
    score_scale = 1.0 / math.sqrt(HD)
    query_heads = queries.reshape(own_rows, local_heads, HD)
    axes = ("blk", "team")
    keys = lax.all_gather(key_rows, axes, axis=0, tiled=True)
    values = lax.all_gather(value_rows, axes, axis=0, tiled=True)
    blocks = keys.shape[0] // own_rows
    keys = keys.reshape(blocks, own_rows, local_heads, HD)
    values = values.reshape(blocks, own_rows, local_heads, HD)

    def one_block(current, block_pair):
        return (attend_block(current, *block_pair, query_heads, score_scale), None)

    (_, row_total, weighted), _ = lax.scan(
        one_block,
        (
            jnp.full((own_rows, local_heads), -1e30, jnp.float32),
            jnp.zeros((own_rows, local_heads), jnp.float32),
            jnp.zeros((own_rows, local_heads, HD), jnp.float32),
        ),
        (keys, values),
    )
    mixed = weighted / row_total[:, :, None]
    return mixed.reshape(own_rows, local_heads * HD).astype(jnp.bfloat16)


def soften(q, k):
    scores = lax.dot_general(
        q, k, (((1,), (1,)), ((), ())), preferred_element_type=jnp.float32
    ) * (1.0 / math.sqrt(HD))
    top = jnp.max(scores, axis=1, keepdims=True)
    weights = jnp.exp(scores - top)
    return weights.astype(jnp.bfloat16), 1.0 / jnp.sum(weights, axis=1, keepdims=True)


def mix(weights, scale, v):
    mixed = jnp.dot(weights, v, preferred_element_type=jnp.float32)
    return (mixed * scale).astype(jnp.bfloat16)


def exchange_kernel(
    blks, teams, cores, whole, rest,
    q_ref, k_ref, v_ref, out_ref,
    qw, kw, vw, ow, weights, qr, kvr, orest,
    send_sem, out_send_sem, recv_sem, direct_sem, passed_sem, rest_q_sem, out_sem,
):
    rows = q_ref.shape[0]
    members = blks * teams
    blk, team, core = lax.axis_index("blk"), lax.axis_index("team"), lax.axis_index("head")
    me = blk * teams + team

    def where(member, on_core=core):
        return {"blk": member // teams, "team": member % teams, "head": on_core}

    def at_rows(block):
        return pl.ds(pl.multiple_of(block * rows, rows), rows)

    def head_cols(head):
        return pl.ds(pl.multiple_of(head * HD, HD), HD)

    steps = sorted(range(1, members), key=lambda s: -min(s, members - s))
    others = [lax.rem(me + s, members) for s in steps]

    barrier = pltpu.get_barrier_semaphore()
    greeted = cores if rest else 1
    for turn in range(greeted):
        on_core = lax.rem(core + turn, cores)
        for other in others + ([me] if turn else []):
            pl.semaphore_signal(
                barrier, inc=1, device_id=where(other, on_core), device_id_type=MESH
            )
    for g in range(whole):
        for a, (src, dst) in enumerate(((k_ref, kw), (q_ref, qw), (v_ref, vw))):
            pltpu.make_async_copy(
                src.at[:, head_cols(me * whole + g)], dst.at[g, at_rows(me), :], recv_sem.at[a]
            ).start()
    pl.semaphore_wait(barrier, members * greeted - 1)

    def put(src, dst, here, device, sends, sem):
        @pl.when(here)
        def _():
            pltpu.make_async_copy(src, dst, sem).start()

        @pl.when(jnp.logical_not(here))
        def _():
            pltpu.make_async_remote_copy(
                src_ref=src, dst_ref=dst, send_sem=sends, recv_sem=sem,
                device_id=device, device_id_type=MESH,
            ).start()

    def arrived(ref, sem):
        pltpu.make_async_copy(ref, ref, sem).wait()

    part, slot = (me // rest, me % rest) if rest else (0, 0)
    for r in range(rest):
        home = core * rest + r
        cols = head_cols(members * whole + r)
        for a, src in enumerate((k_ref, v_ref)):
            put(
                src.at[:, cols], kvr.at[a, at_rows(me), :], home == blk,
                where(home * teams + team), send_sem, direct_sem.at[blk],
            )
        put(
            q_ref.at[:, cols], qr.at[at_rows(slot), :],
            (home == blk) & (part == team * cores + core),
            where(home * teams + part // cores, part % cores), send_sem, rest_q_sem,
        )
    sent = []
    for a, (src, dst) in enumerate(((k_ref, kw), (q_ref, qw), (v_ref, vw))):
        for other in others:
            for g in range(whole):
                copy = pltpu.make_async_remote_copy(
                    src_ref=src.at[:, head_cols(other * whole + g)],
                    dst_ref=dst.at[g, at_rows(me), :],
                    send_sem=send_sem, recv_sem=recv_sem.at[a],
                    device_id=where(other), device_id_type=MESH,
                )
                copy.start()
                sent.append(copy)

    if rest:
        @pl.when(blk // rest == core)
        def _():
            for b in range(blks):
                block = kvr.at[:, at_rows(b * teams + team), :]
                arrived(block, direct_sem.at[b])
                for turn in range(1, teams * cores):
                    t = lax.rem(team + turn // cores, teams)
                    pltpu.make_async_remote_copy(
                        src_ref=block, dst_ref=block, send_sem=send_sem, recv_sem=passed_sem,
                        device_id=where(blk * teams + t, lax.rem(core + turn % cores, cores)),
                        device_id_type=MESH,
                    ).start()

    for a, ref in enumerate((kw, qw)):
        arrived(ref, recv_sem.at[a])
    half = members // 2 * rows
    spans = (slice(0, half), slice(half, members * rows)) if half else (slice(0, rows),)
    scales = []
    for g in range(whole):
        for span in spans:
            weights[g, span, :], scale = soften(qw[g, span, :], kw[g])
            scales.append(scale)
    first = (team * cores + core) * rest
    if rest:
        @pl.when(blk // rest == core)
        def _():
            if teams > 1:
                arrived(kvr.at[:, pl.ds(0, (teams - 1) * blks * rows), :], passed_sem)

        @pl.when(blk // rest != core)
        def _():
            arrived(kvr, passed_sem)

        arrived(qr, rest_q_sem)
        orest[...] = mix(*soften(qr[...], kvr[0]), kvr[1])
        for b in range(rest):
            put(
                orest.at[pl.ds(b * rows, rows), :],
                out_ref.at[:, head_cols(members * whole + blk % rest)],
                (blk // rest == core) & (first + b == me),
                where(first + b, blk // rest), out_send_sem, out_sem,
            )
    arrived(vw, recv_sem.at[2])
    for g in range(whole):
        for span in spans:
            ow[g, span, :] = mix(weights[g, span, :], scales.pop(0), vw[g])
    for g in range(whole):
        for b in range(members):
            put(
                ow.at[g, pl.ds(b * rows, rows), :], out_ref.at[:, head_cols(me * whole + g)],
                b == me, where(b), out_send_sem, out_sem,
            )

    for copy in sent:
        copy.wait_send()
    tile = ow.at[0, pl.ds(0, rows), :]
    for r in range(rest):
        home = core * rest + r

        @pl.when(home != blk)
        def _():
            for _ in range(2):
                arrived(tile, send_sem)

        @pl.when((home != blk) | (part != team * cores + core))
        def _():
            arrived(tile, send_sem)
    if rest:
        @pl.when(blk // rest == core)
        def _():
            for _ in range(teams * cores - 1):
                arrived(kvr.at[:, pl.ds(0, blks * rows), :], send_sem)
    for b in range(members):
        @pl.when(b != me)
        def _():
            arrived(ow.at[:, pl.ds(0, rows), :], out_send_sem)
    for b in range(rest):
        @pl.when((blk // rest != core) | (first + b != me))
        def _():
            arrived(tile, out_send_sem)
    arrived(out_ref, out_sem)


def exchanged(queries, key_rows, value_rows, *, blks, teams, cores, whole, rest):
    rows, columns = queries.shape
    members = blks * teams
    bf16 = jnp.bfloat16
    full = pltpu.VMEM((whole, members * rows, HD), bf16)
    rest_part = pltpu.VMEM((max(rest, 1) * rows, HD), bf16)
    return pl.pallas_call(
        partial(exchange_kernel, blks, teams, cores, whole, rest),
        out_shape=jax.ShapeDtypeStruct((rows, columns), bf16),
        in_specs=[pl.BlockSpec(memory_space=pl.ANY)] * 3,
        out_specs=pl.BlockSpec(memory_space=pl.ANY),
        scratch_shapes=[
            full, full, full, full,
            pltpu.VMEM((whole, members * rows, members * rows), bf16),
            rest_part, pltpu.VMEM((2, members * rows, HD), bf16), rest_part,
            pltpu.SemaphoreType.DMA,
            pltpu.SemaphoreType.DMA,
            pltpu.SemaphoreType.DMA((3,)),
            pltpu.SemaphoreType.DMA((blks,)),
            pltpu.SemaphoreType.DMA,
            pltpu.SemaphoreType.DMA,
            pltpu.SemaphoreType.DMA,
        ],
        compiler_params=pltpu.CompilerParams(collective_id=0, has_side_effects=True),
    )(queries, key_rows, value_rows)


def solution(mesh):
    blks, teams, cores = (mesh.shape[name] for name in ("blk", "team", "head"))

    def local(queries, key_rows, value_rows):
        heads = queries.shape[1] // HD
        whole, rest = heads // (blks * teams), heads % (blks * teams)
        if whole >= 1 and rest * cores in (0, blks):
            return exchanged(
                queries, key_rows, value_rows,
                blks=blks, teams=teams, cores=cores, whole=whole, rest=rest,
            )
        return gathered(queries, key_rows, value_rows)

    spec = P(("groups", "blk", "team"), "head")
    return jax.shard_map(
        local, mesh=mesh, in_specs=(spec,) * 3, out_specs=spec, check_vma=False
    )
```

```python
from functools import partial
import math

import jax
import jax.numpy as jnp
from jax import lax
from jax.experimental import pallas as pl
from jax.experimental.pallas import tpu as pltpu
from jax.sharding import PartitionSpec as P

HD = 128
MESH = pl.DeviceIdType.MESH


def attend_block(running, key_block, value_block, query_rows, score_scale):
    row_top, row_total, weighted = running
    scores = (
        jnp.einsum("qhd,khd->qhk", query_rows, key_block, preferred_element_type=jnp.float32)
        * score_scale
    )
    new_top = jnp.maximum(row_top, jnp.max(scores, axis=2))
    shrink = jnp.exp(row_top - new_top)
    weights = jnp.exp(scores - new_top[:, :, None])
    row_total = row_total * shrink + jnp.sum(weights, axis=2)
    weighted = weighted * shrink[:, :, None] + jnp.einsum(
        "qhk,khd->qhd",
        weights.astype(jnp.bfloat16),
        value_block,
        preferred_element_type=jnp.float32,
    )
    return (new_top, row_total, weighted)


def gathered(queries, key_rows, value_rows):
    own_rows = queries.shape[0]
    local_heads = queries.shape[1] // HD
    score_scale = 1.0 / math.sqrt(HD)
    query_heads = queries.reshape(own_rows, local_heads, HD)
    axes = ("blk", "team")
    keys = lax.all_gather(key_rows, axes, axis=0, tiled=True)
    values = lax.all_gather(value_rows, axes, axis=0, tiled=True)
    blocks = keys.shape[0] // own_rows
    keys = keys.reshape(blocks, own_rows, local_heads, HD)
    values = values.reshape(blocks, own_rows, local_heads, HD)

    def one_block(current, block_pair):
        return (attend_block(current, *block_pair, query_heads, score_scale), None)

    (_, row_total, weighted), _ = lax.scan(
        one_block,
        (
            jnp.full((own_rows, local_heads), -1e30, jnp.float32),
            jnp.zeros((own_rows, local_heads), jnp.float32),
            jnp.zeros((own_rows, local_heads, HD), jnp.float32),
        ),
        (keys, values),
    )
    mixed = weighted / row_total[:, :, None]
    return mixed.reshape(own_rows, local_heads * HD).astype(jnp.bfloat16)


def soften(q, k):
    scores = lax.dot_general(
        q, k, (((1,), (1,)), ((), ())), preferred_element_type=jnp.float32
    ) * (1.0 / math.sqrt(HD))
    top = jnp.max(scores, axis=1, keepdims=True)
    weights = jnp.exp(scores - top)
    return weights.astype(jnp.bfloat16), 1.0 / jnp.sum(weights, axis=1, keepdims=True)


def mix(weights, scale, v):
    mixed = jnp.dot(weights, v, preferred_element_type=jnp.float32)
    return (mixed * scale).astype(jnp.bfloat16)


def exchange_kernel(
    blks, teams, cores, whole, rest,
    q_ref, k_ref, v_ref, out_ref,
    held, got, ow, weights, qr, kvr, orest,
    load_sem, send_sem, out_send_sem, recv_sem, direct_sem, passed_sem, rest_q_sem, out_sem,
):
    rows = q_ref.shape[0]
    members = blks * teams
    blk, team, core = lax.axis_index("blk"), lax.axis_index("team"), lax.axis_index("head")
    me = blk * teams + team

    def where(member, on_core=core):
        return {"blk": member // teams, "team": member % teams, "head": on_core}

    def at_rows(block):
        return pl.ds(pl.multiple_of(block * rows, rows), rows)

    def head_cols(head):
        return pl.ds(pl.multiple_of(head * HD, HD), HD)

    steps = sorted(range(1, members), key=lambda s: -min(s, members - s))
    others = [lax.rem(me + s, members) for s in steps]

    barrier = pltpu.get_barrier_semaphore()
    greeted = cores if rest else 1
    for turn in range(greeted):
        on_core = lax.rem(core + turn, cores)
        for other in others + ([me] if turn else []):
            pl.semaphore_signal(
                barrier, inc=1, device_id=where(other, on_core), device_id_type=MESH
            )
    loads = [
        pltpu.make_async_copy(src, held.at[a], load_sem.at[a])
        for a, src in enumerate((q_ref, k_ref, v_ref))
    ]
    for load in loads:
        load.start()
    for load in loads:
        load.wait()
    for g in range(whole):
        cols = head_cols(me * whole + g)
        for a in range(3):
            got[g, a, at_rows(me), :] = held[a, :, cols]
    pl.semaphore_wait(barrier, members * greeted - 1)

    def put(src, dst, here, device, sends, sem):
        @pl.when(here)
        def _():
            pltpu.make_async_copy(src, dst, sem).start()

        @pl.when(jnp.logical_not(here))
        def _():
            pltpu.make_async_remote_copy(
                src_ref=src, dst_ref=dst, send_sem=sends, recv_sem=sem,
                device_id=device, device_id_type=MESH,
            ).start()

    def arrived(ref, sem):
        pltpu.make_async_copy(ref, ref, sem).wait()

    part, slot = (me // rest, me % rest) if rest else (0, 0)
    for r in range(rest):
        home = core * rest + r
        cols = head_cols(members * whole + r)
        put(
            held.at[pl.ds(1, 2), :, cols], kvr.at[:, at_rows(me), :], home == blk,
            where(home * teams + team), send_sem, direct_sem.at[blk],
        )
        put(
            held.at[0, :, cols], qr.at[at_rows(slot), :],
            (home == blk) & (part == team * cores + core),
            where(home * teams + part // cores, part % cores), send_sem, rest_q_sem,
        )
    sent = []
    for a, kinds in enumerate((pl.ds(0, 2), pl.ds(2, 1))):
        for other in others:
            for g in range(whole):
                copy = pltpu.make_async_remote_copy(
                    src_ref=held.at[kinds, :, head_cols(other * whole + g)],
                    dst_ref=got.at[g, kinds, at_rows(me), :],
                    send_sem=send_sem, recv_sem=recv_sem.at[a],
                    device_id=where(other), device_id_type=MESH,
                )
                copy.start()
                sent.append(copy)

    if rest:
        @pl.when(blk // rest == core)
        def _():
            for b in range(blks):
                block = kvr.at[:, at_rows(b * teams + team), :]
                arrived(block, direct_sem.at[b])
                for turn in range(1, teams * cores):
                    t = lax.rem(team + turn // cores, teams)
                    pltpu.make_async_remote_copy(
                        src_ref=block, dst_ref=block, send_sem=send_sem, recv_sem=passed_sem,
                        device_id=where(blk * teams + t, lax.rem(core + turn % cores, cores)),
                        device_id_type=MESH,
                    ).start()

    far = pl.ds(0, (members - 1) * rows)
    arrived(got.at[:, pl.ds(0, 2), far, :], recv_sem.at[0])
    half = members // 2 * rows
    spans = (slice(0, half), slice(half, members * rows)) if half else (slice(0, rows),)
    scales = []
    for g in range(whole):
        for span in spans:
            weights[g, span, :], scale = soften(got[g, 0, span, :], got[g, 1])
            scales.append(scale)
    first = (team * cores + core) * rest
    if rest:
        @pl.when(blk // rest == core)
        def _():
            if teams > 1:
                arrived(kvr.at[:, pl.ds(0, (teams - 1) * blks * rows), :], passed_sem)

        @pl.when(blk // rest != core)
        def _():
            arrived(kvr, passed_sem)

        arrived(qr, rest_q_sem)
        orest[...] = mix(*soften(qr[...], kvr[0]), kvr[1])
        for b in range(rest):
            put(
                orest.at[pl.ds(b * rows, rows), :],
                out_ref.at[:, head_cols(members * whole + blk % rest)],
                (blk // rest == core) & (first + b == me),
                where(first + b, blk // rest), out_send_sem, out_sem,
            )
    arrived(got.at[:, pl.ds(2, 1), far, :], recv_sem.at[1])
    for g in range(whole):
        for span in spans:
            ow[g, span, :] = mix(weights[g, span, :], scales.pop(0), got[g, 2])
    for g in range(whole):
        for b in range(members):
            put(
                ow.at[g, pl.ds(b * rows, rows), :], out_ref.at[:, head_cols(me * whole + g)],
                b == me, where(b), out_send_sem, out_sem,
            )

    for copy in sent:
        copy.wait_send()
    tile = ow.at[0, pl.ds(0, rows), :]
    for r in range(rest):
        home = core * rest + r

        @pl.when(home != blk)
        def _():
            arrived(kvr.at[:, pl.ds(0, rows), :], send_sem)

        @pl.when((home != blk) | (part != team * cores + core))
        def _():
            arrived(tile, send_sem)
    if rest:
        @pl.when(blk // rest == core)
        def _():
            for _ in range(teams * cores - 1):
                arrived(kvr.at[:, pl.ds(0, blks * rows), :], send_sem)
    for b in range(members):
        @pl.when(b != me)
        def _():
            arrived(ow.at[:, pl.ds(0, rows), :], out_send_sem)
    for b in range(rest):
        @pl.when((blk // rest != core) | (first + b != me))
        def _():
            arrived(tile, out_send_sem)
    arrived(out_ref, out_sem)


def exchanged(queries, key_rows, value_rows, *, blks, teams, cores, whole, rest):
    rows, columns = queries.shape
    members = blks * teams
    bf16 = jnp.bfloat16
    rest_part = pltpu.VMEM((max(rest, 1) * rows, HD), bf16)
    return pl.pallas_call(
        partial(exchange_kernel, blks, teams, cores, whole, rest),
        out_shape=jax.ShapeDtypeStruct((rows, columns), bf16),
        in_specs=[pl.BlockSpec(memory_space=pl.ANY)] * 3,
        out_specs=pl.BlockSpec(memory_space=pl.ANY),
        scratch_shapes=[
            pltpu.VMEM((3, rows, columns), bf16),
            pltpu.VMEM((whole, 3, members * rows, HD), bf16),
            pltpu.VMEM((whole, members * rows, HD), bf16),
            pltpu.VMEM((whole, members * rows, members * rows), bf16),
            rest_part, pltpu.VMEM((2, members * rows, HD), bf16), rest_part,
            pltpu.SemaphoreType.DMA((3,)),
            pltpu.SemaphoreType.DMA,
            pltpu.SemaphoreType.DMA,
            pltpu.SemaphoreType.DMA((2,)),
            pltpu.SemaphoreType.DMA((blks,)),
            pltpu.SemaphoreType.DMA,
            pltpu.SemaphoreType.DMA,
            pltpu.SemaphoreType.DMA,
        ],
        compiler_params=pltpu.CompilerParams(collective_id=0, has_side_effects=True),
    )(queries, key_rows, value_rows)


def solution(mesh):
    blks, teams, cores = (mesh.shape[name] for name in ("blk", "team", "head"))

    def local(queries, key_rows, value_rows):
        heads = queries.shape[1] // HD
        whole, rest = heads // (blks * teams), heads % (blks * teams)
        if whole >= 1 and rest * cores in (0, blks):
            return exchanged(
                queries, key_rows, value_rows,
                blks=blks, teams=teams, cores=cores, whole=whole, rest=rest,
            )
        return gathered(queries, key_rows, value_rows)

    spec = P(("groups", "blk", "team"), "head")
    return jax.shard_map(
        local, mesh=mesh, in_specs=(spec,) * 3, out_specs=spec, check_vma=False
    )
```

```python
from functools import partial
import math

import jax
import jax.numpy as jnp
from jax import lax
from jax.experimental import pallas as pl
from jax.experimental.pallas import tpu as pltpu
from jax.sharding import PartitionSpec as P

HD = 128
MESH = pl.DeviceIdType.MESH


def attend_block(running, key_block, value_block, query_rows, score_scale):
    row_top, row_total, weighted = running
    scores = (
        jnp.einsum("qhd,khd->qhk", query_rows, key_block, preferred_element_type=jnp.float32)
        * score_scale
    )
    new_top = jnp.maximum(row_top, jnp.max(scores, axis=2))
    shrink = jnp.exp(row_top - new_top)
    weights = jnp.exp(scores - new_top[:, :, None])
    row_total = row_total * shrink + jnp.sum(weights, axis=2)
    weighted = weighted * shrink[:, :, None] + jnp.einsum(
        "qhk,khd->qhd",
        weights.astype(jnp.bfloat16),
        value_block,
        preferred_element_type=jnp.float32,
    )
    return (new_top, row_total, weighted)


def gathered(queries, key_rows, value_rows):
    own_rows = queries.shape[0]
    local_heads = queries.shape[1] // HD
    score_scale = 1.0 / math.sqrt(HD)
    query_heads = queries.reshape(own_rows, local_heads, HD)
    axes = ("blk", "team")
    keys = lax.all_gather(key_rows, axes, axis=0, tiled=True)
    values = lax.all_gather(value_rows, axes, axis=0, tiled=True)
    blocks = keys.shape[0] // own_rows
    keys = keys.reshape(blocks, own_rows, local_heads, HD)
    values = values.reshape(blocks, own_rows, local_heads, HD)

    def one_block(current, block_pair):
        return (attend_block(current, *block_pair, query_heads, score_scale), None)

    (_, row_total, weighted), _ = lax.scan(
        one_block,
        (
            jnp.full((own_rows, local_heads), -1e30, jnp.float32),
            jnp.zeros((own_rows, local_heads), jnp.float32),
            jnp.zeros((own_rows, local_heads, HD), jnp.float32),
        ),
        (keys, values),
    )
    mixed = weighted / row_total[:, :, None]
    return mixed.reshape(own_rows, local_heads * HD).astype(jnp.bfloat16)


def soften(q, k):
    scores = lax.dot_general(
        q, k, (((1,), (1,)), ((), ())), preferred_element_type=jnp.float32
    ) * (1.0 / math.sqrt(HD))
    top = jnp.max(scores, axis=1, keepdims=True)
    weights = jnp.exp(scores - top)
    return weights.astype(jnp.bfloat16), 1.0 / jnp.sum(weights, axis=1, keepdims=True)


def mix(weights, scale, v):
    mixed = jnp.dot(weights, v, preferred_element_type=jnp.float32)
    return (mixed * scale).astype(jnp.bfloat16)


def flipped(member, turn, members):
    out, bit = 0, 1
    while bit < members:
        out = out + lax.rem(member // bit + turn // bit, 2) * bit
        bit *= 2
    return out


def exchange_kernel(
    blks, teams, cores, whole, rest,
    q_ref, k_ref, v_ref, out_ref,
    held, got, ow, qr, kvr, orest,
    load_sem, send_sem, out_send_sem, recv_sem, direct_sem, passed_sem, rest_q_sem, out_sem,
):
    rows = q_ref.shape[0]
    members = blks * teams
    blk, team, core = lax.axis_index("blk"), lax.axis_index("team"), lax.axis_index("head")
    me = blk * teams + team

    def where(member, on_core=core):
        return {"blk": member // teams, "team": member % teams, "head": on_core}

    def at_rows(block):
        return pl.ds(pl.multiple_of(block * rows, rows), rows)

    def head_cols(head):
        return pl.ds(pl.multiple_of(head * HD, HD), HD)

    if members & (members - 1) == 0:
        others = sources = [flipped(me, s, members) for s in range(members - 1, 0, -1)]
    else:
        steps = sorted(range(1, members), key=lambda s: -min(s, members - s))
        others = [lax.rem(me + s, members) for s in steps]
        sources = [lax.rem(me + members - s, members) for s in steps]

    barrier = pltpu.get_barrier_semaphore()
    greeted = cores if rest else 1
    for turn in range(greeted):
        on_core = lax.rem(core + turn, cores)
        for other in others + ([me] if turn else []):
            pl.semaphore_signal(
                barrier, inc=1, device_id=where(other, on_core), device_id_type=MESH
            )
    loads = [
        pltpu.make_async_copy(src, held.at[a], load_sem.at[a])
        for a, src in enumerate((q_ref, k_ref, v_ref))
    ]
    for load in loads:
        load.start()
    for load in loads:
        load.wait()
    for g in range(whole):
        cols = head_cols(me * whole + g)
        for a in range(3):
            got[g, a, pl.ds((members - 1) * rows, rows), :] = held[a, :, cols]
    pl.semaphore_wait(barrier, members * greeted - 1)

    def put(src, dst, here, device, sends, sem):
        @pl.when(here)
        def _():
            pltpu.make_async_copy(src, dst, sem).start()

        @pl.when(jnp.logical_not(here))
        def _():
            pltpu.make_async_remote_copy(
                src_ref=src, dst_ref=dst, send_sem=sends, recv_sem=sem,
                device_id=device, device_id_type=MESH,
            ).start()

    def arrived(ref, sem):
        pltpu.make_async_copy(ref, ref, sem).wait()

    part, slot = (me // rest, me % rest) if rest else (0, 0)
    for r in range(rest):
        home = core * rest + r
        cols = head_cols(members * whole + r)
        put(
            held.at[pl.ds(1, 2), :, cols], kvr.at[:, at_rows(me), :], home == blk,
            where(home * teams + team), send_sem, direct_sem.at[blk],
        )
        put(
            held.at[0, :, cols], qr.at[at_rows(slot), :],
            (home == blk) & (part == team * cores + core),
            where(home * teams + part // cores, part % cores), send_sem, rest_q_sem,
        )
    sent = []
    far, last = members // 2, members - 1
    all_heads = pl.ds(0, whole)
    legs = ((0, 2, 0, far), (1, 2, far, last), (2, 3, 0, last), (0, 1, far, last))
    for leg, (low, high, start, stop) in enumerate(legs):
        for i in range(start, stop):
            for g in range(whole):
                copy = pltpu.make_async_remote_copy(
                    src_ref=held.at[pl.ds(low, high - low), :, head_cols(others[i] * whole + g)],
                    dst_ref=got.at[g, pl.ds(low, high - low), pl.ds(i * rows, rows), :],
                    send_sem=send_sem, recv_sem=recv_sem.at[leg],
                    device_id=where(others[i]), device_id_type=MESH,
                )
                copy.start()
                sent.append(copy)

    def leg_arrived(leg):
        low, high, start, stop = legs[leg]
        if stop > start:
            span = pl.ds(start * rows, (stop - start) * rows)
            arrived(got.at[all_heads, pl.ds(low, high - low), span, :], recv_sem.at[leg])

    if rest:
        @pl.when(blk // rest == core)
        def _():
            for b in range(blks):
                block = kvr.at[:, at_rows(b * teams + team), :]
                arrived(block, direct_sem.at[b])
                for turn in range(1, teams * cores):
                    t = lax.rem(team + turn // cores, teams)
                    pltpu.make_async_remote_copy(
                        src_ref=block, dst_ref=block, send_sem=send_sem, recv_sem=passed_sem,
                        device_id=where(blk * teams + t, lax.rem(core + turn % cores, cores)),
                        device_id_type=MESH,
                    ).start()

    first = (team * cores + core) * rest
    if rest:
        @pl.when(blk // rest == core)
        def _():
            if teams > 1:
                arrived(kvr.at[:, pl.ds(0, (teams - 1) * blks * rows), :], passed_sem)

        @pl.when(blk // rest != core)
        def _():
            arrived(kvr, passed_sem)

        arrived(qr, rest_q_sem)
        orest[...] = mix(*soften(qr[...], kvr[0]), kvr[1])
        for b in range(rest):
            put(
                orest.at[pl.ds(b * rows, rows), :],
                out_ref.at[:, head_cols(members * whole + blk % rest)],
                (blk // rest == core) & (first + b == me),
                where(first + b, blk // rest), out_send_sem, out_sem,
            )

    def soften_slots(g, start, stop):
        return soften(got[g, 0, pl.ds(start * rows, (stop - start) * rows), :], got[g, 1])

    def give_slots(g, start, stop, weights, scale):
        ow[g, pl.ds(start * rows, (stop - start) * rows), :] = mix(weights, scale, got[g, 2])
        for i in range(start, stop):
            src = ow.at[g, pl.ds(i * rows, rows), :]
            dst = out_ref.at[:, head_cols(me * whole + g)]
            if i == last:
                pltpu.make_async_copy(src, dst, out_sem).start()
            else:
                pltpu.make_async_remote_copy(
                    src_ref=src, dst_ref=dst, send_sem=out_send_sem, recv_sem=out_sem,
                    device_id=where(sources[i]), device_id_type=MESH,
                ).start()

    leg_arrived(0)
    leg_arrived(1)
    softened = [soften_slots(g, 0, far) for g in range(whole)]
    leg_arrived(2)
    for g in range(whole):
        give_slots(g, 0, far, *softened[g])
    leg_arrived(3)
    for g in range(whole):
        give_slots(g, far, members, *soften_slots(g, far, members))

    for copy in sent:
        copy.wait_send()
    tile = ow.at[0, pl.ds(0, rows), :]
    for r in range(rest):
        home = core * rest + r

        @pl.when(home != blk)
        def _():
            arrived(kvr.at[:, pl.ds(0, rows), :], send_sem)

        @pl.when((home != blk) | (part != team * cores + core))
        def _():
            arrived(tile, send_sem)
    if rest:
        @pl.when(blk // rest == core)
        def _():
            for _ in range(teams * cores - 1):
                arrived(kvr.at[:, pl.ds(0, blks * rows), :], send_sem)
    arrived(ow.at[:, pl.ds(0, last * rows), :], out_send_sem)
    for b in range(rest):
        @pl.when((blk // rest != core) | (first + b != me))
        def _():
            arrived(tile, out_send_sem)
    arrived(out_ref, out_sem)


def exchanged(queries, key_rows, value_rows, *, blks, teams, cores, whole, rest):
    rows, columns = queries.shape
    members = blks * teams
    bf16 = jnp.bfloat16
    rest_part = pltpu.VMEM((max(rest, 1) * rows, HD), bf16)
    return pl.pallas_call(
        partial(exchange_kernel, blks, teams, cores, whole, rest),
        out_shape=jax.ShapeDtypeStruct((rows, columns), bf16),
        in_specs=[pl.BlockSpec(memory_space=pl.ANY)] * 3,
        out_specs=pl.BlockSpec(memory_space=pl.ANY),
        scratch_shapes=[
            pltpu.VMEM((3, rows, columns), bf16),
            pltpu.VMEM((whole, 3, members * rows, HD), bf16),
            pltpu.VMEM((whole, members * rows, HD), bf16),
            rest_part, pltpu.VMEM((2, members * rows, HD), bf16), rest_part,
            pltpu.SemaphoreType.DMA((3,)),
            pltpu.SemaphoreType.DMA,
            pltpu.SemaphoreType.DMA,
            pltpu.SemaphoreType.DMA((4,)),
            pltpu.SemaphoreType.DMA((blks,)),
            pltpu.SemaphoreType.DMA,
            pltpu.SemaphoreType.DMA,
            pltpu.SemaphoreType.DMA,
        ],
        compiler_params=pltpu.CompilerParams(collective_id=0, has_side_effects=True),
    )(queries, key_rows, value_rows)


def solution(mesh):
    blks, teams, cores = (mesh.shape[name] for name in ("blk", "team", "head"))

    def local(queries, key_rows, value_rows):
        heads = queries.shape[1] // HD
        whole, rest = heads // (blks * teams), heads % (blks * teams)
        if whole >= 1 and blks * teams >= 2 and rest * cores in (0, blks):
            return exchanged(
                queries, key_rows, value_rows,
                blks=blks, teams=teams, cores=cores, whole=whole, rest=rest,
            )
        return gathered(queries, key_rows, value_rows)

    spec = P(("groups", "blk", "team"), "head")
    return jax.shard_map(
        local, mesh=mesh, in_specs=(spec,) * 3, out_specs=spec, check_vma=False
    )
```

```python
from functools import partial
import math

import jax
import jax.numpy as jnp
from jax import lax
from jax.experimental import pallas as pl
from jax.experimental.pallas import tpu as pltpu
from jax.sharding import PartitionSpec as P

HD = 128
MESH = pl.DeviceIdType.MESH


def attend_block(running, key_block, value_block, query_rows, score_scale):
    row_top, row_total, weighted = running
    scores = (
        jnp.einsum("qhd,khd->qhk", query_rows, key_block, preferred_element_type=jnp.float32)
        * score_scale
    )
    new_top = jnp.maximum(row_top, jnp.max(scores, axis=2))
    shrink = jnp.exp(row_top - new_top)
    weights = jnp.exp(scores - new_top[:, :, None])
    row_total = row_total * shrink + jnp.sum(weights, axis=2)
    weighted = weighted * shrink[:, :, None] + jnp.einsum(
        "qhk,khd->qhd",
        weights.astype(jnp.bfloat16),
        value_block,
        preferred_element_type=jnp.float32,
    )
    return (new_top, row_total, weighted)


def gathered(queries, key_rows, value_rows):
    own_rows = queries.shape[0]
    local_heads = queries.shape[1] // HD
    score_scale = 1.0 / math.sqrt(HD)
    query_heads = queries.reshape(own_rows, local_heads, HD)
    axes = ("blk", "team")
    keys = lax.all_gather(key_rows, axes, axis=0, tiled=True)
    values = lax.all_gather(value_rows, axes, axis=0, tiled=True)
    blocks = keys.shape[0] // own_rows
    keys = keys.reshape(blocks, own_rows, local_heads, HD)
    values = values.reshape(blocks, own_rows, local_heads, HD)

    def one_block(current, block_pair):
        return (attend_block(current, *block_pair, query_heads, score_scale), None)

    (_, row_total, weighted), _ = lax.scan(
        one_block,
        (
            jnp.full((own_rows, local_heads), -1e30, jnp.float32),
            jnp.zeros((own_rows, local_heads), jnp.float32),
            jnp.zeros((own_rows, local_heads, HD), jnp.float32),
        ),
        (keys, values),
    )
    mixed = weighted / row_total[:, :, None]
    return mixed.reshape(own_rows, local_heads * HD).astype(jnp.bfloat16)


def soften(q, k):
    scores = lax.dot_general(
        q, k, (((1,), (1,)), ((), ())), preferred_element_type=jnp.float32
    ) * (1.0 / math.sqrt(HD))
    top = jnp.max(scores, axis=1, keepdims=True)
    weights = jnp.exp(scores - top)
    return weights.astype(jnp.bfloat16), 1.0 / jnp.sum(weights, axis=1, keepdims=True)


def mix(weights, scale, v):
    mixed = jnp.dot(weights, v, preferred_element_type=jnp.float32)
    return (mixed * scale).astype(jnp.bfloat16)


def flipped(member, turn, members):
    out, bit = 0, 1
    while bit < members:
        out = out + lax.rem(member // bit + turn // bit, 2) * bit
        bit *= 2
    return out


def exchange_kernel(
    blks, teams, cores, whole, rest,
    q_ref, k_ref, v_ref, out_ref,
    held, got, ow, qr, kvr, orest,
    load_sem, send_sem, out_send_sem, recv_sem, direct_sem, passed_sem, rest_q_sem, out_sem,
):
    rows = q_ref.shape[0]
    members = blks * teams
    blk, team, core = lax.axis_index("blk"), lax.axis_index("team"), lax.axis_index("head")
    me = blk * teams + team

    def where(member, on_core=core):
        return {"blk": member // teams, "team": member % teams, "head": on_core}

    def at_rows(block):
        return pl.ds(pl.multiple_of(block * rows, rows), rows)

    def head_cols(head):
        return pl.ds(pl.multiple_of(head * HD, HD), HD)

    if members & (members - 1) == 0:
        others = sources = [flipped(me, s, members) for s in range(members - 1, 0, -1)]
    else:
        steps = sorted(range(1, members), key=lambda s: -min(s, members - s))
        others = [lax.rem(me + s, members) for s in steps]
        sources = [lax.rem(me + members - s, members) for s in steps]

    barrier = pltpu.get_barrier_semaphore()
    greeted = cores if rest else 1
    for turn in range(greeted):
        on_core = lax.rem(core + turn, cores)
        for other in others + ([me] if turn else []):
            pl.semaphore_signal(
                barrier, inc=1, device_id=where(other, on_core), device_id_type=MESH
            )
    loads = [
        pltpu.make_async_copy(src, held.at[a], load_sem.at[a])
        for a, src in enumerate((q_ref, k_ref, v_ref))
    ]
    for load in loads:
        load.start()
    for load in loads:
        load.wait()
    for g in range(whole):
        cols = head_cols(me * whole + g)
        for a in range(3):
            got[g, a, pl.ds((members - 1) * rows, rows), :] = held[a, :, cols]
    pl.semaphore_wait(barrier, members * greeted - 1)

    def put(src, dst, here, device, sends, sem):
        @pl.when(here)
        def _():
            pltpu.make_async_copy(src, dst, sem).start()

        @pl.when(jnp.logical_not(here))
        def _():
            pltpu.make_async_remote_copy(
                src_ref=src, dst_ref=dst, send_sem=sends, recv_sem=sem,
                device_id=device, device_id_type=MESH,
            ).start()

    def arrived(ref, sem):
        pltpu.make_async_copy(ref, ref, sem).wait()

    part, slot = (me // rest, me % rest) if rest else (0, 0)
    for r in range(rest):
        home = core * rest + r
        cols = head_cols(members * whole + r)
        put(
            held.at[pl.ds(1, 2), :, cols], kvr.at[:, at_rows(me), :], home == blk,
            where(home * teams + team), send_sem, direct_sem.at[blk],
        )
        put(
            held.at[0, :, cols], qr.at[at_rows(slot), :],
            (home == blk) & (part == team * cores + core),
            where(home * teams + part // cores, part % cores), send_sem, rest_q_sem,
        )
    sent = []
    last = members - 1
    all_heads = pl.ds(0, whole)

    def send_leg(leg, kinds):
        for i in range(last):
            for g in range(whole):
                copy = pltpu.make_async_remote_copy(
                    src_ref=held.at[kinds, :, head_cols(others[i] * whole + g)],
                    dst_ref=got.at[g, kinds, pl.ds(i * rows, rows), :],
                    send_sem=send_sem, recv_sem=recv_sem.at[leg],
                    device_id=where(others[i]), device_id_type=MESH,
                )
                copy.start()
                sent.append(copy)

    def leg_arrived(leg, kinds):
        arrived(got.at[all_heads, kinds, pl.ds(0, last * rows), :], recv_sem.at[leg])

    queries_keys, values = pl.ds(0, 2), pl.ds(2, 1)
    send_leg(0, queries_keys)
    if rest:
        @pl.when(blk // rest == core)
        def _():
            for b in range(blks):
                block = kvr.at[:, at_rows(b * teams + team), :]
                arrived(block, direct_sem.at[b])
                for turn in range(1, teams * cores):
                    t = lax.rem(team + turn // cores, teams)
                    pltpu.make_async_remote_copy(
                        src_ref=block, dst_ref=block, send_sem=send_sem, recv_sem=passed_sem,
                        device_id=where(blk * teams + t, lax.rem(core + turn % cores, cores)),
                        device_id_type=MESH,
                    ).start()

    send_leg(1, values)

    leg_arrived(0, queries_keys)
    half = members // 2 * rows
    softened = [
        [soften(got[g, 0, span, :], got[g, 1]) for span in (slice(0, half), slice(half, members * rows))]
        for g in range(whole)
    ]
    first = (team * cores + core) * rest
    if rest:
        @pl.when(blk // rest == core)
        def _():
            if teams > 1:
                arrived(kvr.at[:, pl.ds(0, (teams - 1) * blks * rows), :], passed_sem)

        @pl.when(blk // rest != core)
        def _():
            arrived(kvr, passed_sem)

        arrived(qr, rest_q_sem)
        orest[...] = mix(*soften(qr[...], kvr[0]), kvr[1])
        for b in range(rest):
            put(
                orest.at[pl.ds(b * rows, rows), :],
                out_ref.at[:, head_cols(members * whole + blk % rest)],
                (blk // rest == core) & (first + b == me),
                where(first + b, blk // rest), out_send_sem, out_sem,
            )

    leg_arrived(1, values)
    for g in range(whole):
        for start, (weights, scale) in zip((0, half), softened[g]):
            ow[g, pl.ds(start, weights.shape[0]), :] = mix(weights, scale, got[g, 2])
    for g in range(whole):
        for i in range(members):
            src = ow.at[g, pl.ds(i * rows, rows), :]
            dst = out_ref.at[:, head_cols(me * whole + g)]
            if i == last:
                pltpu.make_async_copy(src, dst, out_sem).start()
            else:
                pltpu.make_async_remote_copy(
                    src_ref=src, dst_ref=dst, send_sem=out_send_sem, recv_sem=out_sem,
                    device_id=where(sources[i]), device_id_type=MESH,
                ).start()

    for copy in sent:
        copy.wait_send()
    tile = ow.at[0, pl.ds(0, rows), :]
    for r in range(rest):
        home = core * rest + r

        @pl.when(home != blk)
        def _():
            arrived(kvr.at[:, pl.ds(0, rows), :], send_sem)

        @pl.when((home != blk) | (part != team * cores + core))
        def _():
            arrived(tile, send_sem)
    if rest:
        @pl.when(blk // rest == core)
        def _():
            for _ in range(teams * cores - 1):
                arrived(kvr.at[:, pl.ds(0, blks * rows), :], send_sem)
    arrived(ow.at[:, pl.ds(0, last * rows), :], out_send_sem)
    for b in range(rest):
        @pl.when((blk // rest != core) | (first + b != me))
        def _():
            arrived(tile, out_send_sem)
    arrived(out_ref, out_sem)


def exchanged(queries, key_rows, value_rows, *, blks, teams, cores, whole, rest):
    rows, columns = queries.shape
    members = blks * teams
    bf16 = jnp.bfloat16
    rest_part = pltpu.VMEM((max(rest, 1) * rows, HD), bf16)
    return pl.pallas_call(
        partial(exchange_kernel, blks, teams, cores, whole, rest),
        out_shape=jax.ShapeDtypeStruct((rows, columns), bf16),
        in_specs=[pl.BlockSpec(memory_space=pl.ANY)] * 3,
        out_specs=pl.BlockSpec(memory_space=pl.ANY),
        scratch_shapes=[
            pltpu.VMEM((3, rows, columns), bf16),
            pltpu.VMEM((whole, 3, members * rows, HD), bf16),
            pltpu.VMEM((whole, members * rows, HD), bf16),
            rest_part, pltpu.VMEM((2, members * rows, HD), bf16), rest_part,
            pltpu.SemaphoreType.DMA((3,)),
            pltpu.SemaphoreType.DMA,
            pltpu.SemaphoreType.DMA,
            pltpu.SemaphoreType.DMA((2,)),
            pltpu.SemaphoreType.DMA((blks,)),
            pltpu.SemaphoreType.DMA,
            pltpu.SemaphoreType.DMA,
            pltpu.SemaphoreType.DMA,
        ],
        compiler_params=pltpu.CompilerParams(collective_id=0, has_side_effects=True),
    )(queries, key_rows, value_rows)


def solution(mesh):
    blks, teams, cores = (mesh.shape[name] for name in ("blk", "team", "head"))

    def local(queries, key_rows, value_rows):
        heads = queries.shape[1] // HD
        whole, rest = heads // (blks * teams), heads % (blks * teams)
        if whole >= 1 and blks * teams >= 2 and rest * cores in (0, blks):
            return exchanged(
                queries, key_rows, value_rows,
                blks=blks, teams=teams, cores=cores, whole=whole, rest=rest,
            )
        return gathered(queries, key_rows, value_rows)

    spec = P(("groups", "blk", "team"), "head")
    return jax.shard_map(
        local, mesh=mesh, in_specs=(spec,) * 3, out_specs=spec, check_vma=False
    )
```

```python
from functools import partial
import math

import jax
import jax.numpy as jnp
from jax import lax
from jax.experimental import pallas as pl
from jax.experimental.pallas import tpu as pltpu
from jax.sharding import PartitionSpec as P

HD = 128
MESH = pl.DeviceIdType.MESH


def attend_block(running, key_block, value_block, query_rows, score_scale):
    row_top, row_total, weighted = running
    scores = (
        jnp.einsum("qhd,khd->qhk", query_rows, key_block, preferred_element_type=jnp.float32)
        * score_scale
    )
    new_top = jnp.maximum(row_top, jnp.max(scores, axis=2))
    shrink = jnp.exp(row_top - new_top)
    weights = jnp.exp(scores - new_top[:, :, None])
    row_total = row_total * shrink + jnp.sum(weights, axis=2)
    weighted = weighted * shrink[:, :, None] + jnp.einsum(
        "qhk,khd->qhd",
        weights.astype(jnp.bfloat16),
        value_block,
        preferred_element_type=jnp.float32,
    )
    return (new_top, row_total, weighted)


def gathered(queries, key_rows, value_rows):
    own_rows = queries.shape[0]
    local_heads = queries.shape[1] // HD
    score_scale = 1.0 / math.sqrt(HD)
    query_heads = queries.reshape(own_rows, local_heads, HD)
    axes = ("blk", "team")
    keys = lax.all_gather(key_rows, axes, axis=0, tiled=True)
    values = lax.all_gather(value_rows, axes, axis=0, tiled=True)
    blocks = keys.shape[0] // own_rows
    keys = keys.reshape(blocks, own_rows, local_heads, HD)
    values = values.reshape(blocks, own_rows, local_heads, HD)

    def one_block(current, block_pair):
        return (attend_block(current, *block_pair, query_heads, score_scale), None)

    (_, row_total, weighted), _ = lax.scan(
        one_block,
        (
            jnp.full((own_rows, local_heads), -1e30, jnp.float32),
            jnp.zeros((own_rows, local_heads), jnp.float32),
            jnp.zeros((own_rows, local_heads, HD), jnp.float32),
        ),
        (keys, values),
    )
    mixed = weighted / row_total[:, :, None]
    return mixed.reshape(own_rows, local_heads * HD).astype(jnp.bfloat16)


def soften(q, k):
    scores = lax.dot_general(
        q, k, (((1,), (1,)), ((), ())), preferred_element_type=jnp.float32
    ) * (1.0 / math.sqrt(HD))
    top = jnp.max(scores, axis=1, keepdims=True)
    weights = jnp.exp(scores - top)
    return weights.astype(jnp.bfloat16), 1.0 / jnp.sum(weights, axis=1, keepdims=True)


def mix(weights, scale, v):
    mixed = jnp.dot(weights, v, preferred_element_type=jnp.float32)
    return (mixed * scale).astype(jnp.bfloat16)


def flipped(member, turn, members):
    out, bit = 0, 1
    while bit < members:
        out = out + lax.rem(member // bit + turn // bit, 2) * bit
        bit *= 2
    return out


def exchange_kernel(
    blks, teams, cores, whole, rest,
    q_ref, k_ref, v_ref, out_ref,
    held, got, ow, shared, orest,
    load_sem, send_sem, out_send_sem, recv_sem, direct_sem, passed_sem, out_sem,
):
    rows = q_ref.shape[0]
    members = blks * teams
    blk, team, core = lax.axis_index("blk"), lax.axis_index("team"), lax.axis_index("head")
    me = blk * teams + team

    def where(member, on_core=core):
        return {"blk": member // teams, "team": member % teams, "head": on_core}

    def at_rows(block):
        return pl.ds(pl.multiple_of(block * rows, rows), rows)

    def head_cols(head):
        return pl.ds(pl.multiple_of(head * HD, HD), HD)

    if members & (members - 1) == 0:
        others = sources = [flipped(me, s, members) for s in range(members - 1, 0, -1)]
    else:
        steps = sorted(range(1, members), key=lambda s: -min(s, members - s))
        others = [lax.rem(me + s, members) for s in steps]
        sources = [lax.rem(me + members - s, members) for s in steps]

    helper, owner = cores - 1, (blk // rest if rest else 0)

    barrier = pltpu.get_barrier_semaphore()

    def greet(member, on_core):
        pl.semaphore_signal(
            barrier, inc=1, device_id=where(member, on_core), device_id_type=MESH
        )

    for other in others:
        greet(other, core)
    if rest and cores > 1:
        @pl.when(core != helper)
        def _():
            for r in range(rest):
                greet((core * rest + r) * teams + team, helper)

        @pl.when((core == helper) & (owner != helper))
        def _():
            for b in range(blks):
                greet(b * teams + team, owner)

    loads = [
        pltpu.make_async_copy(src, held.at[a], load_sem.at[a])
        for a, src in enumerate((q_ref, k_ref, v_ref))
    ]
    for load in loads:
        load.start()
    for load in loads:
        load.wait()
    for g in range(whole):
        cols = head_cols(me * whole + g)
        for a in range(3):
            got[g, a, pl.ds((members - 1) * rows, rows), :] = held[a, :, cols]
    greeted = members - 1
    if rest and cores > 1:
        greeted = greeted + jnp.where(core != helper, rest, jnp.where(owner != helper, blks, 0))
    pl.semaphore_wait(barrier, greeted)

    def put(src, dst, here, device, sends, sem):
        @pl.when(here)
        def _():
            pltpu.make_async_copy(src, dst, sem).start()

        @pl.when(jnp.logical_not(here))
        def _():
            pltpu.make_async_remote_copy(
                src_ref=src, dst_ref=dst, send_sem=sends, recv_sem=sem,
                device_id=device, device_id_type=MESH,
            ).start()

    def arrived(ref, sem):
        pltpu.make_async_copy(ref, ref, sem).wait()

    for r in range(rest):
        home = core * rest + r
        put(
            held.at[:, :, head_cols(members * whole + r)], shared.at[:, at_rows(blk), :],
            (home == blk) & (core == helper), where(home * teams + team, helper),
            send_sem, direct_sem.at[blk],
        )
    sent = []
    last = members - 1
    all_heads = pl.ds(0, whole)

    def send_leg(leg, kinds):
        for i in range(last):
            for g in range(whole):
                copy = pltpu.make_async_remote_copy(
                    src_ref=held.at[kinds, :, head_cols(others[i] * whole + g)],
                    dst_ref=got.at[g, kinds, pl.ds(i * rows, rows), :],
                    send_sem=send_sem, recv_sem=recv_sem.at[leg],
                    device_id=where(others[i]), device_id_type=MESH,
                )
                copy.start()
                sent.append(copy)

    def leg_arrived(leg, kinds):
        arrived(got.at[all_heads, kinds, pl.ds(0, last * rows), :], recv_sem.at[leg])

    queries_keys, keys_values, values = pl.ds(0, 2), pl.ds(1, 2), pl.ds(2, 1)
    send_leg(0, queries_keys)
    if rest:
        @pl.when(core == helper)
        def _():
            for b in range(blks):
                arrived(shared.at[:, pl.ds(b * rows, rows), :], direct_sem.at[b])
                for turn in range(1, teams):
                    pltpu.make_async_remote_copy(
                        src_ref=shared.at[keys_values, pl.ds(b * rows, rows), :],
                        dst_ref=shared.at[keys_values, pl.ds((turn * blks + b) * rows, rows), :],
                        send_sem=send_sem, recv_sem=passed_sem,
                        device_id=where(blk * teams + lax.rem(team + turn, teams)),
                        device_id_type=MESH,
                    ).start()

    send_leg(1, values)

    leg_arrived(0, queries_keys)
    half = members // 2 * rows
    softened = [
        [soften(got[g, 0, span, :], got[g, 1]) for span in (slice(0, half), slice(half, members * rows))]
        for g in range(whole)
    ]
    passed = shared.at[keys_values, pl.ds(0, (teams - 1) * blks * rows), :]
    if rest:
        @pl.when(core == helper)
        def _():
            if teams > 1:
                arrived(passed, passed_sem)
            mine = shared[0, pl.ds(0, blks * rows), :]
            orest[...] = mix(*soften(mine, shared[1]), shared[2])
            for b in range(blks):
                put(
                    orest.at[pl.ds(b * rows, rows), :],
                    out_ref.at[:, head_cols(members * whole + blk % rest)],
                    (owner == helper) & (b == blk), where(b * teams + team, owner),
                    out_send_sem, out_sem,
                )

    leg_arrived(1, values)
    for g in range(whole):
        for start, (weights, scale) in zip((0, half), softened[g]):
            ow[g, pl.ds(start, weights.shape[0]), :] = mix(weights, scale, got[g, 2])
    for g in range(whole):
        for i in range(members):
            src = ow.at[g, pl.ds(i * rows, rows), :]
            dst = out_ref.at[:, head_cols(me * whole + g)]
            if i == last:
                pltpu.make_async_copy(src, dst, out_sem).start()
            else:
                pltpu.make_async_remote_copy(
                    src_ref=src, dst_ref=dst, send_sem=out_send_sem, recv_sem=out_sem,
                    device_id=where(sources[i]), device_id_type=MESH,
                ).start()

    for copy in sent:
        copy.wait_send()
    for r in range(rest):
        @pl.when((core * rest + r != blk) | (core != helper))
        def _():
            arrived(shared.at[:, pl.ds(0, rows), :], send_sem)
    arrived(ow.at[:, pl.ds(0, last * rows), :], out_send_sem)
    if rest:
        @pl.when(core == helper)
        def _():
            if teams > 1:
                arrived(passed, send_sem)
            for b in range(blks):
                @pl.when((owner != helper) | (b != blk))
                def _():
                    arrived(orest.at[pl.ds(b * rows, rows), :], out_send_sem)
    arrived(out_ref, out_sem)


def exchanged(queries, key_rows, value_rows, *, blks, teams, cores, whole, rest):
    rows, columns = queries.shape
    members = blks * teams
    bf16 = jnp.bfloat16
    return pl.pallas_call(
        partial(exchange_kernel, blks, teams, cores, whole, rest),
        out_shape=jax.ShapeDtypeStruct((rows, columns), bf16),
        in_specs=[pl.BlockSpec(memory_space=pl.ANY)] * 3,
        out_specs=pl.BlockSpec(memory_space=pl.ANY),
        scratch_shapes=[
            pltpu.VMEM((3, rows, columns), bf16),
            pltpu.VMEM((whole, 3, members * rows, HD), bf16),
            pltpu.VMEM((whole, members * rows, HD), bf16),
            pltpu.VMEM((3, members * rows, HD), bf16),
            pltpu.VMEM((blks * rows, HD), bf16),
            pltpu.SemaphoreType.DMA((3,)),
            pltpu.SemaphoreType.DMA,
            pltpu.SemaphoreType.DMA,
            pltpu.SemaphoreType.DMA((2,)),
            pltpu.SemaphoreType.DMA((blks,)),
            pltpu.SemaphoreType.DMA,
            pltpu.SemaphoreType.DMA,
        ],
        compiler_params=pltpu.CompilerParams(collective_id=0, has_side_effects=True),
    )(queries, key_rows, value_rows)


def solution(mesh):
    blks, teams, cores = (mesh.shape[name] for name in ("blk", "team", "head"))

    def local(queries, key_rows, value_rows):
        heads = queries.shape[1] // HD
        whole, rest = heads // (blks * teams), heads % (blks * teams)
        if whole >= 1 and blks * teams >= 2 and rest * cores in (0, blks):
            return exchanged(
                queries, key_rows, value_rows,
                blks=blks, teams=teams, cores=cores, whole=whole, rest=rest,
            )
        return gathered(queries, key_rows, value_rows)

    spec = P(("groups", "blk", "team"), "head")
    return jax.shard_map(
        local, mesh=mesh, in_specs=(spec,) * 3, out_specs=spec, check_vma=False
    )
```

```python
from functools import partial
import math

import jax
import jax.numpy as jnp
from jax import lax
from jax.experimental import pallas as pl
from jax.experimental.pallas import tpu as pltpu
from jax.sharding import PartitionSpec as P

HD = 128
MESH = pl.DeviceIdType.MESH


def attend_block(running, key_block, value_block, query_rows, score_scale):
    row_top, row_total, weighted = running
    scores = (
        jnp.einsum("qhd,khd->qhk", query_rows, key_block, preferred_element_type=jnp.float32)
        * score_scale
    )
    new_top = jnp.maximum(row_top, jnp.max(scores, axis=2))
    shrink = jnp.exp(row_top - new_top)
    weights = jnp.exp(scores - new_top[:, :, None])
    row_total = row_total * shrink + jnp.sum(weights, axis=2)
    weighted = weighted * shrink[:, :, None] + jnp.einsum(
        "qhk,khd->qhd",
        weights.astype(jnp.bfloat16),
        value_block,
        preferred_element_type=jnp.float32,
    )
    return (new_top, row_total, weighted)


def gathered(queries, key_rows, value_rows):
    own_rows = queries.shape[0]
    local_heads = queries.shape[1] // HD
    score_scale = 1.0 / math.sqrt(HD)
    query_heads = queries.reshape(own_rows, local_heads, HD)
    axes = ("blk", "team")
    keys = lax.all_gather(key_rows, axes, axis=0, tiled=True)
    values = lax.all_gather(value_rows, axes, axis=0, tiled=True)
    blocks = keys.shape[0] // own_rows
    keys = keys.reshape(blocks, own_rows, local_heads, HD)
    values = values.reshape(blocks, own_rows, local_heads, HD)

    def one_block(current, block_pair):
        return (attend_block(current, *block_pair, query_heads, score_scale), None)

    (_, row_total, weighted), _ = lax.scan(
        one_block,
        (
            jnp.full((own_rows, local_heads), -1e30, jnp.float32),
            jnp.zeros((own_rows, local_heads), jnp.float32),
            jnp.zeros((own_rows, local_heads, HD), jnp.float32),
        ),
        (keys, values),
    )
    mixed = weighted / row_total[:, :, None]
    return mixed.reshape(own_rows, local_heads * HD).astype(jnp.bfloat16)


def soften(q, k):
    scores = lax.dot_general(
        q, k, (((1,), (1,)), ((), ())), preferred_element_type=jnp.float32
    ) * (1.0 / math.sqrt(HD))
    top = jnp.max(scores, axis=1, keepdims=True)
    weights = jnp.exp(scores - top)
    return weights.astype(jnp.bfloat16), 1.0 / jnp.sum(weights, axis=1, keepdims=True)


def mix(weights, scale, v):
    mixed = jnp.dot(weights, v, preferred_element_type=jnp.float32)
    return (mixed * scale).astype(jnp.bfloat16)


def flipped(member, turn, members):
    out, bit = 0, 1
    while bit < members:
        out = out + lax.rem(member // bit + turn // bit, 2) * bit
        bit *= 2
    return out


def exchange_kernel(
    blks, teams, cores, whole, rest,
    q_ref, k_ref, v_ref, out_ref,
    held, got, ow, shared, orest,
    load_sem, send_sem, out_send_sem, recv_sem, direct_sem, passed_sem, out_sem,
):
    rows = q_ref.shape[0]
    members = blks * teams
    blk, team, core = lax.axis_index("blk"), lax.axis_index("team"), lax.axis_index("head")
    me = blk * teams + team

    def where(member, on_core=core):
        return {"blk": member // teams, "team": member % teams, "head": on_core}

    def at_rows(block):
        return pl.ds(pl.multiple_of(block * rows, rows), rows)

    def head_cols(head):
        return pl.ds(pl.multiple_of(head * HD, HD), HD)

    if members & (members - 1) == 0:
        others = [flipped(me, s, members) for s in range(members - 1, 0, -1)]
    else:
        steps = sorted(range(1, members), key=lambda s: -min(s, members - s))
        others = [lax.rem(me + s, members) for s in steps]

    helper, owner = cores - 1, (blk // rest if rest else 0)

    loads = [
        pltpu.make_async_copy(src, held.at[a], load_sem.at[a])
        for a, src in enumerate((q_ref, k_ref, v_ref))
    ]
    for load in loads:
        load.start()
    barrier = pltpu.get_barrier_semaphore()

    def greet(member, on_core):
        pl.semaphore_signal(
            barrier, inc=1, device_id=where(member, on_core), device_id_type=MESH
        )

    for other in others:
        greet(other, core)
    if rest and cores > 1:
        @pl.when(core != helper)
        def _():
            for r in range(rest):
                greet((core * rest + r) * teams + team, helper)

        @pl.when((core == helper) & (owner != helper))
        def _():
            for b in range(blks):
                greet(b * teams + team, owner)

    for load in loads:
        load.wait()
    greeted = members - 1
    if rest and cores > 1:
        greeted = greeted + jnp.where(core != helper, rest, jnp.where(owner != helper, blks, 0))
    pl.semaphore_wait(barrier, greeted)

    def put(src, dst, here, device, sends, sem):
        @pl.when(here)
        def _():
            pltpu.make_async_copy(src, dst, sem).start()

        @pl.when(jnp.logical_not(here))
        def _():
            pltpu.make_async_remote_copy(
                src_ref=src, dst_ref=dst, send_sem=sends, recv_sem=sem,
                device_id=device, device_id_type=MESH,
            ).start()

    def arrived(ref, sem):
        pltpu.make_async_copy(ref, ref, sem).wait()

    for r in range(rest):
        home = core * rest + r
        put(
            held.at[:, :, head_cols(members * whole + r)], shared.at[:, at_rows(blk), :],
            (home == blk) & (core == helper), where(home * teams + team, helper),
            send_sem, direct_sem.at[blk],
        )
    sent = []
    last = members - 1
    all_heads = pl.ds(0, whole)

    def send_leg(leg, kinds):
        for i in range(last):
            for g in range(whole):
                copy = pltpu.make_async_remote_copy(
                    src_ref=held.at[kinds, :, head_cols(others[i] * whole + g)],
                    dst_ref=got.at[g, kinds, at_rows(me), :],
                    send_sem=send_sem, recv_sem=recv_sem.at[leg],
                    device_id=where(others[i]), device_id_type=MESH,
                )
                copy.start()
                sent.append(copy)

    def leg_arrived(leg, kinds):
        arrived(got.at[all_heads, kinds, pl.ds(0, last * rows), :], recv_sem.at[leg])

    queries_keys, keys_values, values = pl.ds(0, 2), pl.ds(1, 2), pl.ds(2, 1)
    send_leg(0, queries_keys)
    if rest:
        @pl.when(core == helper)
        def _():
            for b in range(blks):
                arrived(shared.at[:, pl.ds(b * rows, rows), :], direct_sem.at[b])
                for turn in range(1, teams):
                    pltpu.make_async_remote_copy(
                        src_ref=shared.at[keys_values, pl.ds(b * rows, rows), :],
                        dst_ref=shared.at[keys_values, pl.ds((turn * blks + b) * rows, rows), :],
                        send_sem=send_sem, recv_sem=passed_sem,
                        device_id=where(blk * teams + lax.rem(team + turn, teams)),
                        device_id_type=MESH,
                    ).start()

    send_leg(1, values)

    for g in range(whole):
        for a in range(3):
            got[g, a, at_rows(me), :] = held[a, :, head_cols(me * whole + g)]
    leg_arrived(0, queries_keys)
    half = members // 2 * rows
    softened = [
        [soften(got[g, 0, span, :], got[g, 1]) for span in (slice(0, half), slice(half, members * rows))]
        for g in range(whole)
    ]
    passed = shared.at[keys_values, pl.ds(0, (teams - 1) * blks * rows), :]
    if rest:
        @pl.when(core == helper)
        def _():
            if teams > 1:
                arrived(passed, passed_sem)
            mine = shared[0, pl.ds(0, blks * rows), :]
            orest[...] = mix(*soften(mine, shared[1]), shared[2])
            for b in range(blks):
                put(
                    orest.at[pl.ds(b * rows, rows), :],
                    out_ref.at[:, head_cols(members * whole + blk % rest)],
                    (owner == helper) & (b == blk), where(b * teams + team, owner),
                    out_send_sem, out_sem,
                )

    leg_arrived(1, values)
    for g in range(whole):
        for start, (weights, scale) in zip((0, half), softened[g]):
            ow[g, pl.ds(start, weights.shape[0]), :] = mix(weights, scale, got[g, 2])
    for g in range(whole):
        for b in range(members):
            put(
                ow.at[g, pl.ds(b * rows, rows), :], out_ref.at[:, head_cols(me * whole + g)],
                b == me, where(b), out_send_sem, out_sem,
            )

    for copy in sent:
        copy.wait_send()
    for r in range(rest):
        @pl.when((core * rest + r != blk) | (core != helper))
        def _():
            arrived(shared.at[:, pl.ds(0, rows), :], send_sem)
    arrived(ow.at[:, pl.ds(0, last * rows), :], out_send_sem)
    if rest:
        @pl.when(core == helper)
        def _():
            if teams > 1:
                arrived(passed, send_sem)
            for b in range(blks):
                @pl.when((owner != helper) | (b != blk))
                def _():
                    arrived(orest.at[pl.ds(b * rows, rows), :], out_send_sem)
    arrived(out_ref, out_sem)


def exchanged(queries, key_rows, value_rows, *, blks, teams, cores, whole, rest):
    rows, columns = queries.shape
    members = blks * teams
    bf16 = jnp.bfloat16
    return pl.pallas_call(
        partial(exchange_kernel, blks, teams, cores, whole, rest),
        out_shape=jax.ShapeDtypeStruct((rows, columns), bf16),
        in_specs=[pl.BlockSpec(memory_space=pl.ANY)] * 3,
        out_specs=pl.BlockSpec(memory_space=pl.ANY),
        scratch_shapes=[
            pltpu.VMEM((3, rows, columns), bf16),
            pltpu.VMEM((whole, 3, members * rows, HD), bf16),
            pltpu.VMEM((whole, members * rows, HD), bf16),
            pltpu.VMEM((3, members * rows, HD), bf16),
            pltpu.VMEM((blks * rows, HD), bf16),
            pltpu.SemaphoreType.DMA((3,)),
            pltpu.SemaphoreType.DMA,
            pltpu.SemaphoreType.DMA,
            pltpu.SemaphoreType.DMA((2,)),
            pltpu.SemaphoreType.DMA((blks,)),
            pltpu.SemaphoreType.DMA,
            pltpu.SemaphoreType.DMA,
        ],
        compiler_params=pltpu.CompilerParams(collective_id=0, has_side_effects=True),
    )(queries, key_rows, value_rows)


def solution(mesh):
    blks, teams, cores = (mesh.shape[name] for name in ("blk", "team", "head"))

    def local(queries, key_rows, value_rows):
        heads = queries.shape[1] // HD
        whole, rest = heads // (blks * teams), heads % (blks * teams)
        if whole >= 1 and blks * teams >= 2 and rest * cores in (0, blks):
            return exchanged(
                queries, key_rows, value_rows,
                blks=blks, teams=teams, cores=cores, whole=whole, rest=rest,
            )
        return gathered(queries, key_rows, value_rows)

    spec = P(("groups", "blk", "team"), "head")
    return jax.shard_map(
        local, mesh=mesh, in_specs=(spec,) * 3, out_specs=spec, check_vma=False
    )
```

```python
from functools import partial
import math

import jax
import jax.numpy as jnp
from jax import lax
from jax.experimental import pallas as pl
from jax.experimental.pallas import tpu as pltpu
from jax.sharding import PartitionSpec as P

HD = 128
MESH = pl.DeviceIdType.MESH


def attend_block(running, key_block, value_block, query_rows, score_scale):
    row_top, row_total, weighted = running
    scores = (
        jnp.einsum("qhd,khd->qhk", query_rows, key_block, preferred_element_type=jnp.float32)
        * score_scale
    )
    new_top = jnp.maximum(row_top, jnp.max(scores, axis=2))
    shrink = jnp.exp(row_top - new_top)
    weights = jnp.exp(scores - new_top[:, :, None])
    row_total = row_total * shrink + jnp.sum(weights, axis=2)
    weighted = weighted * shrink[:, :, None] + jnp.einsum(
        "qhk,khd->qhd",
        weights.astype(jnp.bfloat16),
        value_block,
        preferred_element_type=jnp.float32,
    )
    return (new_top, row_total, weighted)


def gathered(queries, key_rows, value_rows):
    own_rows = queries.shape[0]
    local_heads = queries.shape[1] // HD
    score_scale = 1.0 / math.sqrt(HD)
    query_heads = queries.reshape(own_rows, local_heads, HD)
    axes = ("blk", "team")
    keys = lax.all_gather(key_rows, axes, axis=0, tiled=True)
    values = lax.all_gather(value_rows, axes, axis=0, tiled=True)
    blocks = keys.shape[0] // own_rows
    keys = keys.reshape(blocks, own_rows, local_heads, HD)
    values = values.reshape(blocks, own_rows, local_heads, HD)

    def one_block(current, block_pair):
        return (attend_block(current, *block_pair, query_heads, score_scale), None)

    (_, row_total, weighted), _ = lax.scan(
        one_block,
        (
            jnp.full((own_rows, local_heads), -1e30, jnp.float32),
            jnp.zeros((own_rows, local_heads), jnp.float32),
            jnp.zeros((own_rows, local_heads, HD), jnp.float32),
        ),
        (keys, values),
    )
    mixed = weighted / row_total[:, :, None]
    return mixed.reshape(own_rows, local_heads * HD).astype(jnp.bfloat16)


def soften(q, k):
    scores = lax.dot_general(
        q, k, (((1,), (1,)), ((), ())), preferred_element_type=jnp.float32
    ) * (1.0 / math.sqrt(HD))
    top = jnp.max(scores, axis=1, keepdims=True)
    weights = jnp.exp(scores - top)
    return weights.astype(jnp.bfloat16), 1.0 / jnp.sum(weights, axis=1, keepdims=True)


def mix(weights, scale, v):
    mixed = jnp.dot(weights, v, preferred_element_type=jnp.float32)
    return (mixed * scale).astype(jnp.bfloat16)


def flipped(member, turn, members):
    out, bit = 0, 1
    while bit < members:
        out = out + lax.rem(member // bit + turn // bit, 2) * bit
        bit *= 2
    return out


def exchange_kernel(
    blks, teams, cores, whole, rest,
    q_ref, k_ref, v_ref, out_ref,
    staged, held, got, ow, shared, orest,
    load_sem, send_sem, out_send_sem, recv_sem, direct_sem, passed_sem, out_sem,
):
    rows = q_ref.shape[0]
    members = blks * teams
    blk, team, core = lax.axis_index("blk"), lax.axis_index("team"), lax.axis_index("head")
    me = blk * teams + team

    def where(member, on_core=core):
        return {"blk": member // teams, "team": member % teams, "head": on_core}

    def at_rows(block):
        return pl.ds(pl.multiple_of(block * rows, rows), rows)

    def head_cols(head):
        return pl.ds(pl.multiple_of(head * HD, HD), HD)

    if members & (members - 1) == 0:
        others = [flipped(me, s, members) for s in range(members - 1, 0, -1)]
    else:
        steps = sorted(range(1, members), key=lambda s: -min(s, members - s))
        others = [lax.rem(me + s, members) for s in steps]

    helper, owner = cores - 1, (blk // rest if rest else 0)

    loads = [
        pltpu.make_async_copy(src, staged.at[a], load_sem.at[a])
        for a, src in enumerate((q_ref, k_ref, v_ref))
    ]
    for load in loads:
        load.start()
    barrier = pltpu.get_barrier_semaphore()

    def greet(member, on_core):
        pl.semaphore_signal(
            barrier, inc=1, device_id=where(member, on_core), device_id_type=MESH
        )

    for other in others:
        greet(other, core)
    if rest and cores > 1:
        @pl.when(core != helper)
        def _():
            for r in range(rest):
                greet((core * rest + r) * teams + team, helper)

        @pl.when((core == helper) & (owner != helper))
        def _():
            for b in range(blks):
                greet(b * teams + team, owner)

    for a, load in enumerate(loads):
        load.wait()
        for head in range(members * whole + rest):
            held[head, a] = staged[a, :, pl.ds(head * HD, HD)]
    greeted = members - 1
    if rest and cores > 1:
        greeted = greeted + jnp.where(core != helper, rest, jnp.where(owner != helper, blks, 0))
    pl.semaphore_wait(barrier, greeted)

    def put(src, dst, here, device, sends, sem):
        @pl.when(here)
        def _():
            pltpu.make_async_copy(src, dst, sem).start()

        @pl.when(jnp.logical_not(here))
        def _():
            pltpu.make_async_remote_copy(
                src_ref=src, dst_ref=dst, send_sem=sends, recv_sem=sem,
                device_id=device, device_id_type=MESH,
            ).start()

    def arrived(ref, sem):
        pltpu.make_async_copy(ref, ref, sem).wait()

    for r in range(rest):
        home = core * rest + r
        put(
            held.at[members * whole + r], shared.at[:, at_rows(blk), :],
            (home == blk) & (core == helper), where(home * teams + team, helper),
            send_sem, direct_sem.at[blk],
        )
    sent = []
    last = members - 1
    all_heads = pl.ds(0, whole)

    def send_leg(leg, kinds):
        for i in range(last):
            for g in range(whole):
                copy = pltpu.make_async_remote_copy(
                    src_ref=held.at[others[i] * whole + g, kinds],
                    dst_ref=got.at[g, kinds, at_rows(me), :],
                    send_sem=send_sem, recv_sem=recv_sem.at[leg],
                    device_id=where(others[i]), device_id_type=MESH,
                )
                copy.start()
                sent.append(copy)

    def leg_arrived(leg, kinds):
        arrived(got.at[all_heads, kinds, pl.ds(0, last * rows), :], recv_sem.at[leg])

    queries_keys, keys_values, values = pl.ds(0, 2), pl.ds(1, 2), pl.ds(2, 1)
    send_leg(0, queries_keys)
    if rest:
        @pl.when(core == helper)
        def _():
            for b in range(blks):
                arrived(shared.at[:, pl.ds(b * rows, rows), :], direct_sem.at[b])
                for turn in range(1, teams):
                    pltpu.make_async_remote_copy(
                        src_ref=shared.at[keys_values, pl.ds(b * rows, rows), :],
                        dst_ref=shared.at[keys_values, pl.ds((turn * blks + b) * rows, rows), :],
                        send_sem=send_sem, recv_sem=passed_sem,
                        device_id=where(blk * teams + lax.rem(team + turn, teams)),
                        device_id_type=MESH,
                    ).start()

    send_leg(1, values)

    for g in range(whole):
        for a in range(3):
            got[g, a, at_rows(me), :] = held[me * whole + g, a]
    leg_arrived(0, queries_keys)
    half = members // 2 * rows
    softened = [
        [soften(got[g, 0, span, :], got[g, 1]) for span in (slice(0, half), slice(half, members * rows))]
        for g in range(whole)
    ]
    passed = shared.at[keys_values, pl.ds(0, (teams - 1) * blks * rows), :]
    if rest:
        @pl.when(core == helper)
        def _():
            if teams > 1:
                arrived(passed, passed_sem)
            mine = shared[0, pl.ds(0, blks * rows), :]
            orest[...] = mix(*soften(mine, shared[1]), shared[2])
            for b in range(blks):
                put(
                    orest.at[pl.ds(b * rows, rows), :],
                    out_ref.at[:, head_cols(members * whole + blk % rest)],
                    (owner == helper) & (b == blk), where(b * teams + team, owner),
                    out_send_sem, out_sem,
                )

    leg_arrived(1, values)
    for g in range(whole):
        for start, (weights, scale) in zip((0, half), softened[g]):
            ow[g, pl.ds(start, weights.shape[0]), :] = mix(weights, scale, got[g, 2])
    for g in range(whole):
        for b in range(members):
            put(
                ow.at[g, pl.ds(b * rows, rows), :], out_ref.at[:, head_cols(me * whole + g)],
                b == me, where(b), out_send_sem, out_sem,
            )

    for copy in sent:
        copy.wait_send()
    for r in range(rest):
        @pl.when((core * rest + r != blk) | (core != helper))
        def _():
            arrived(shared.at[:, pl.ds(0, rows), :], send_sem)
    arrived(ow.at[:, pl.ds(0, last * rows), :], out_send_sem)
    if rest:
        @pl.when(core == helper)
        def _():
            if teams > 1:
                arrived(passed, send_sem)
            for b in range(blks):
                @pl.when((owner != helper) | (b != blk))
                def _():
                    arrived(orest.at[pl.ds(b * rows, rows), :], out_send_sem)
    arrived(out_ref, out_sem)


def exchanged(queries, key_rows, value_rows, *, blks, teams, cores, whole, rest):
    rows, columns = queries.shape
    members = blks * teams
    bf16 = jnp.bfloat16
    return pl.pallas_call(
        partial(exchange_kernel, blks, teams, cores, whole, rest),
        out_shape=jax.ShapeDtypeStruct((rows, columns), bf16),
        in_specs=[pl.BlockSpec(memory_space=pl.ANY)] * 3,
        out_specs=pl.BlockSpec(memory_space=pl.ANY),
        scratch_shapes=[
            pltpu.VMEM((3, rows, columns), bf16),
            pltpu.VMEM((columns // HD, 3, rows, HD), bf16),
            pltpu.VMEM((whole, 3, members * rows, HD), bf16),
            pltpu.VMEM((whole, members * rows, HD), bf16),
            pltpu.VMEM((3, members * rows, HD), bf16),
            pltpu.VMEM((blks * rows, HD), bf16),
            pltpu.SemaphoreType.DMA((3,)),
            pltpu.SemaphoreType.DMA,
            pltpu.SemaphoreType.DMA,
            pltpu.SemaphoreType.DMA((2,)),
            pltpu.SemaphoreType.DMA((blks,)),
            pltpu.SemaphoreType.DMA,
            pltpu.SemaphoreType.DMA,
        ],
        compiler_params=pltpu.CompilerParams(collective_id=0, has_side_effects=True),
    )(queries, key_rows, value_rows)


def solution(mesh):
    blks, teams, cores = (mesh.shape[name] for name in ("blk", "team", "head"))

    def local(queries, key_rows, value_rows):
        heads = queries.shape[1] // HD
        whole, rest = heads // (blks * teams), heads % (blks * teams)
        if whole >= 1 and blks * teams >= 2 and rest * cores in (0, blks):
            return exchanged(
                queries, key_rows, value_rows,
                blks=blks, teams=teams, cores=cores, whole=whole, rest=rest,
            )
        return gathered(queries, key_rows, value_rows)

    spec = P(("groups", "blk", "team"), "head")
    return jax.shard_map(
        local, mesh=mesh, in_specs=(spec,) * 3, out_specs=spec, check_vma=False
    )
```

```python
from functools import partial
import math

import jax
import jax.numpy as jnp
from jax import lax
from jax.experimental import pallas as pl
from jax.experimental.pallas import tpu as pltpu
from jax.sharding import PartitionSpec as P

HD = 128
MESH = pl.DeviceIdType.MESH


def attend_block(running, key_block, value_block, query_rows, score_scale):
    row_top, row_total, weighted = running
    scores = (
        jnp.einsum("qhd,khd->qhk", query_rows, key_block, preferred_element_type=jnp.float32)
        * score_scale
    )
    new_top = jnp.maximum(row_top, jnp.max(scores, axis=2))
    shrink = jnp.exp(row_top - new_top)
    weights = jnp.exp(scores - new_top[:, :, None])
    row_total = row_total * shrink + jnp.sum(weights, axis=2)
    weighted = weighted * shrink[:, :, None] + jnp.einsum(
        "qhk,khd->qhd",
        weights.astype(jnp.bfloat16),
        value_block,
        preferred_element_type=jnp.float32,
    )
    return (new_top, row_total, weighted)


def gathered(queries, key_rows, value_rows):
    own_rows = queries.shape[0]
    local_heads = queries.shape[1] // HD
    score_scale = 1.0 / math.sqrt(HD)
    query_heads = queries.reshape(own_rows, local_heads, HD)
    axes = ("blk", "team")
    keys = lax.all_gather(key_rows, axes, axis=0, tiled=True)
    values = lax.all_gather(value_rows, axes, axis=0, tiled=True)
    blocks = keys.shape[0] // own_rows
    keys = keys.reshape(blocks, own_rows, local_heads, HD)
    values = values.reshape(blocks, own_rows, local_heads, HD)

    def one_block(current, block_pair):
        return (attend_block(current, *block_pair, query_heads, score_scale), None)

    (_, row_total, weighted), _ = lax.scan(
        one_block,
        (
            jnp.full((own_rows, local_heads), -1e30, jnp.float32),
            jnp.zeros((own_rows, local_heads), jnp.float32),
            jnp.zeros((own_rows, local_heads, HD), jnp.float32),
        ),
        (keys, values),
    )
    mixed = weighted / row_total[:, :, None]
    return mixed.reshape(own_rows, local_heads * HD).astype(jnp.bfloat16)


def soften(q, k):
    scores = lax.dot_general(
        q, k, (((1,), (1,)), ((), ())), preferred_element_type=jnp.float32
    ) * (1.0 / math.sqrt(HD))
    top = jnp.max(scores, axis=1, keepdims=True)
    weights = jnp.exp(scores - top)
    return weights.astype(jnp.bfloat16), 1.0 / jnp.sum(weights, axis=1, keepdims=True)


def mix(weights, scale, v):
    mixed = jnp.dot(weights, v, preferred_element_type=jnp.float32)
    return (mixed * scale).astype(jnp.bfloat16)


def flipped(member, turn, members):
    out, bit = 0, 1
    while bit < members:
        out = out + lax.rem(member // bit + turn // bit, 2) * bit
        bit *= 2
    return out


def exchange_kernel(
    blks, teams, cores, whole, rest,
    q_ref, k_ref, v_ref, out_ref,
    staged, held, got, ow, shared, orest,
    load_sem, send_sem, out_send_sem, recv_sem, direct_sem, passed_sem, out_sem,
):
    rows = q_ref.shape[0]
    members = blks * teams
    blk, team, core = lax.axis_index("blk"), lax.axis_index("team"), lax.axis_index("head")
    me = blk * teams + team

    def where(member, on_core=core):
        return {"blk": member // teams, "team": member % teams, "head": on_core}

    def at_rows(block):
        return pl.ds(pl.multiple_of(block * rows, rows), rows)

    def head_cols(head):
        return pl.ds(pl.multiple_of(head * HD, HD), HD)

    if members & (members - 1) == 0:
        others = [flipped(me, s, members) for s in range(members - 1, 0, -1)]
    else:
        steps = sorted(range(1, members), key=lambda s: -min(s, members - s))
        others = [lax.rem(me + s, members) for s in steps]
    others = [
        jnp.where(lax.rem(core, 2) == 0, near, far) for near, far in zip(reversed(others), others)
    ]

    helper, owner = cores - 1, (blk // rest if rest else 0)

    loads = [
        pltpu.make_async_copy(src, staged.at[a], load_sem.at[a])
        for a, src in enumerate((q_ref, k_ref, v_ref))
    ]
    for load in loads:
        load.start()
    barrier = pltpu.get_barrier_semaphore()

    def greet(member, on_core):
        pl.semaphore_signal(
            barrier, inc=1, device_id=where(member, on_core), device_id_type=MESH
        )

    for other in others:
        greet(other, core)
    if rest and cores > 1:
        @pl.when(core != helper)
        def _():
            for r in range(rest):
                greet((core * rest + r) * teams + team, helper)

        @pl.when((core == helper) & (owner != helper))
        def _():
            for b in range(blks):
                greet(b * teams + team, owner)

    for a, load in enumerate(loads):
        load.wait()
        for head in range(members * whole + rest):
            held[head, a] = staged[a, :, pl.ds(head * HD, HD)]
    greeted = members - 1
    if rest and cores > 1:
        greeted = greeted + jnp.where(core != helper, rest, jnp.where(owner != helper, blks, 0))
    pl.semaphore_wait(barrier, greeted)

    def put(src, dst, here, device, sends, sem):
        @pl.when(here)
        def _():
            pltpu.make_async_copy(src, dst, sem).start()

        @pl.when(jnp.logical_not(here))
        def _():
            pltpu.make_async_remote_copy(
                src_ref=src, dst_ref=dst, send_sem=sends, recv_sem=sem,
                device_id=device, device_id_type=MESH,
            ).start()

    def arrived(ref, sem):
        pltpu.make_async_copy(ref, ref, sem).wait()

    for r in range(rest):
        home = core * rest + r
        put(
            held.at[members * whole + r], shared.at[:, at_rows(blk), :],
            (home == blk) & (core == helper), where(home * teams + team, helper),
            send_sem, direct_sem.at[blk],
        )
    sent = []
    last = members - 1
    all_heads = pl.ds(0, whole)

    def send_leg(leg, kinds):
        for i in range(last):
            for g in range(whole):
                copy = pltpu.make_async_remote_copy(
                    src_ref=held.at[others[i] * whole + g, kinds],
                    dst_ref=got.at[g, kinds, at_rows(me), :],
                    send_sem=send_sem, recv_sem=recv_sem.at[leg],
                    device_id=where(others[i]), device_id_type=MESH,
                )
                copy.start()
                sent.append(copy)

    def leg_arrived(leg, kinds):
        arrived(got.at[all_heads, kinds, pl.ds(0, last * rows), :], recv_sem.at[leg])

    queries_keys, keys_values, values = pl.ds(0, 2), pl.ds(1, 2), pl.ds(2, 1)
    send_leg(0, queries_keys)
    if rest:
        @pl.when(core == helper)
        def _():
            for b in range(blks):
                arrived(shared.at[:, pl.ds(b * rows, rows), :], direct_sem.at[b])
                for turn in range(1, teams):
                    pltpu.make_async_remote_copy(
                        src_ref=shared.at[keys_values, pl.ds(b * rows, rows), :],
                        dst_ref=shared.at[keys_values, pl.ds((turn * blks + b) * rows, rows), :],
                        send_sem=send_sem, recv_sem=passed_sem,
                        device_id=where(blk * teams + lax.rem(team + turn, teams)),
                        device_id_type=MESH,
                    ).start()

    send_leg(1, values)

    for g in range(whole):
        for a in range(3):
            got[g, a, at_rows(me), :] = held[me * whole + g, a]
    leg_arrived(0, queries_keys)
    half = members // 2 * rows
    softened = [
        [soften(got[g, 0, span, :], got[g, 1]) for span in (slice(0, half), slice(half, members * rows))]
        for g in range(whole)
    ]
    passed = shared.at[keys_values, pl.ds(0, (teams - 1) * blks * rows), :]
    if rest:
        @pl.when(core == helper)
        def _():
            if teams > 1:
                arrived(passed, passed_sem)
            mine = shared[0, pl.ds(0, blks * rows), :]
            orest[...] = mix(*soften(mine, shared[1]), shared[2])
            for b in range(blks):
                put(
                    orest.at[pl.ds(b * rows, rows), :],
                    out_ref.at[:, head_cols(members * whole + blk % rest)],
                    (owner == helper) & (b == blk), where(b * teams + team, owner),
                    out_send_sem, out_sem,
                )

    leg_arrived(1, values)
    for g in range(whole):
        for start, (weights, scale) in zip((0, half), softened[g]):
            ow[g, pl.ds(start, weights.shape[0]), :] = mix(weights, scale, got[g, 2])
    for g in range(whole):
        for b in range(members):
            put(
                ow.at[g, pl.ds(b * rows, rows), :], out_ref.at[:, head_cols(me * whole + g)],
                b == me, where(b), out_send_sem, out_sem,
            )

    for copy in sent:
        copy.wait_send()
    for r in range(rest):
        @pl.when((core * rest + r != blk) | (core != helper))
        def _():
            arrived(shared.at[:, pl.ds(0, rows), :], send_sem)
    arrived(ow.at[:, pl.ds(0, last * rows), :], out_send_sem)
    if rest:
        @pl.when(core == helper)
        def _():
            if teams > 1:
                arrived(passed, send_sem)
            for b in range(blks):
                @pl.when((owner != helper) | (b != blk))
                def _():
                    arrived(orest.at[pl.ds(b * rows, rows), :], out_send_sem)
    arrived(out_ref, out_sem)


def exchanged(queries, key_rows, value_rows, *, blks, teams, cores, whole, rest):
    rows, columns = queries.shape
    members = blks * teams
    bf16 = jnp.bfloat16
    return pl.pallas_call(
        partial(exchange_kernel, blks, teams, cores, whole, rest),
        out_shape=jax.ShapeDtypeStruct((rows, columns), bf16),
        in_specs=[pl.BlockSpec(memory_space=pl.ANY)] * 3,
        out_specs=pl.BlockSpec(memory_space=pl.ANY),
        scratch_shapes=[
            pltpu.VMEM((3, rows, columns), bf16),
            pltpu.VMEM((columns // HD, 3, rows, HD), bf16),
            pltpu.VMEM((whole, 3, members * rows, HD), bf16),
            pltpu.VMEM((whole, members * rows, HD), bf16),
            pltpu.VMEM((3, members * rows, HD), bf16),
            pltpu.VMEM((blks * rows, HD), bf16),
            pltpu.SemaphoreType.DMA((3,)),
            pltpu.SemaphoreType.DMA,
            pltpu.SemaphoreType.DMA,
            pltpu.SemaphoreType.DMA((2,)),
            pltpu.SemaphoreType.DMA((blks,)),
            pltpu.SemaphoreType.DMA,
            pltpu.SemaphoreType.DMA,
        ],
        compiler_params=pltpu.CompilerParams(collective_id=0, has_side_effects=True),
    )(queries, key_rows, value_rows)


def solution(mesh):
    blks, teams, cores = (mesh.shape[name] for name in ("blk", "team", "head"))

    def local(queries, key_rows, value_rows):
        heads = queries.shape[1] // HD
        whole, rest = heads // (blks * teams), heads % (blks * teams)
        if whole >= 1 and blks * teams >= 2 and rest * cores in (0, blks):
            return exchanged(
                queries, key_rows, value_rows,
                blks=blks, teams=teams, cores=cores, whole=whole, rest=rest,
            )
        return gathered(queries, key_rows, value_rows)

    spec = P(("groups", "blk", "team"), "head")
    return jax.shard_map(
        local, mesh=mesh, in_specs=(spec,) * 3, out_specs=spec, check_vma=False
    )
```

```python
from functools import partial
import math

import jax
import jax.numpy as jnp
from jax import lax
from jax.experimental import pallas as pl
from jax.experimental.pallas import tpu as pltpu
from jax.sharding import PartitionSpec as P

HD = 128
MESH = pl.DeviceIdType.MESH


def attend_block(running, key_block, value_block, query_rows, score_scale):
    row_top, row_total, weighted = running
    scores = (
        jnp.einsum("qhd,khd->qhk", query_rows, key_block, preferred_element_type=jnp.float32)
        * score_scale
    )
    new_top = jnp.maximum(row_top, jnp.max(scores, axis=2))
    shrink = jnp.exp(row_top - new_top)
    weights = jnp.exp(scores - new_top[:, :, None])
    row_total = row_total * shrink + jnp.sum(weights, axis=2)
    weighted = weighted * shrink[:, :, None] + jnp.einsum(
        "qhk,khd->qhd",
        weights.astype(jnp.bfloat16),
        value_block,
        preferred_element_type=jnp.float32,
    )
    return (new_top, row_total, weighted)


def gathered(queries, key_rows, value_rows):
    own_rows = queries.shape[0]
    local_heads = queries.shape[1] // HD
    score_scale = 1.0 / math.sqrt(HD)
    query_heads = queries.reshape(own_rows, local_heads, HD)
    axes = ("blk", "team")
    keys = lax.all_gather(key_rows, axes, axis=0, tiled=True)
    values = lax.all_gather(value_rows, axes, axis=0, tiled=True)
    blocks = keys.shape[0] // own_rows
    keys = keys.reshape(blocks, own_rows, local_heads, HD)
    values = values.reshape(blocks, own_rows, local_heads, HD)

    def one_block(current, block_pair):
        return (attend_block(current, *block_pair, query_heads, score_scale), None)

    (_, row_total, weighted), _ = lax.scan(
        one_block,
        (
            jnp.full((own_rows, local_heads), -1e30, jnp.float32),
            jnp.zeros((own_rows, local_heads), jnp.float32),
            jnp.zeros((own_rows, local_heads, HD), jnp.float32),
        ),
        (keys, values),
    )
    mixed = weighted / row_total[:, :, None]
    return mixed.reshape(own_rows, local_heads * HD).astype(jnp.bfloat16)


def soften(q, k):
    scores = lax.dot_general(
        q, k, (((1,), (1,)), ((), ())), preferred_element_type=jnp.float32
    ) * (1.0 / math.sqrt(HD))
    top = jnp.max(scores, axis=1, keepdims=True)
    weights = jnp.exp(scores - top)
    return weights.astype(jnp.bfloat16), 1.0 / jnp.sum(weights, axis=1, keepdims=True)


def mix(weights, scale, v):
    mixed = jnp.dot(weights, v, preferred_element_type=jnp.float32)
    return (mixed * scale).astype(jnp.bfloat16)


def flipped(member, turn, members):
    out, bit = 0, 1
    while bit < members:
        out = out + lax.rem(member // bit + turn // bit, 2) * bit
        bit *= 2
    return out


def exchange_kernel(
    blks, teams, cores, whole, rest,
    q_ref, k_ref, v_ref, out_ref,
    staged, held, got, ow, shared, orest,
    load_sem, send_sem, out_send_sem, recv_sem, direct_sem, passed_sem, out_sem,
):
    rows = q_ref.shape[0]
    members = blks * teams
    blk, team, core = lax.axis_index("blk"), lax.axis_index("team"), lax.axis_index("head")
    me = blk * teams + team

    def where(member, on_core=core):
        return {"blk": member // teams, "team": member % teams, "head": on_core}

    def at_rows(block):
        return pl.ds(pl.multiple_of(block * rows, rows), rows)

    def head_cols(head):
        return pl.ds(pl.multiple_of(head * HD, HD), HD)

    if members & (members - 1) == 0:
        others = [flipped(me, s, members) for s in range(members - 1, 0, -1)]
    else:
        steps = sorted(range(1, members), key=lambda s: -min(s, members - s))
        others = [lax.rem(me + s, members) for s in steps]

    helper, owner = cores - 1, (blk // rest if rest else 0)

    loads = [
        pltpu.make_async_copy(src, staged.at[a], load_sem.at[a])
        for a, src in enumerate((q_ref, k_ref, v_ref))
    ]
    for load in loads:
        load.start()
    barrier = pltpu.get_barrier_semaphore()

    def greet(member, on_core):
        pl.semaphore_signal(
            barrier, inc=1, device_id=where(member, on_core), device_id_type=MESH
        )

    for other in others:
        greet(other, core)
    if rest and cores > 1:
        @pl.when(core != helper)
        def _():
            for r in range(rest):
                greet((core * rest + r) * teams + team, helper)

        @pl.when((core == helper) & (owner != helper))
        def _():
            for b in range(blks):
                greet(b * teams + team, owner)

    for a, load in enumerate(loads):
        load.wait()
        for head in range(members * whole + rest):
            held[head, a] = staged[a, :, pl.ds(head * HD, HD)]
    greeted = members - 1
    if rest and cores > 1:
        greeted = greeted + jnp.where(core != helper, rest, jnp.where(owner != helper, blks, 0))
    pl.semaphore_wait(barrier, greeted)

    def put(src, dst, here, device, sends, sem):
        @pl.when(here)
        def _():
            pltpu.make_async_copy(src, dst, sem).start()

        @pl.when(jnp.logical_not(here))
        def _():
            pltpu.make_async_remote_copy(
                src_ref=src, dst_ref=dst, send_sem=sends, recv_sem=sem,
                device_id=device, device_id_type=MESH,
            ).start()

    def arrived(ref, sem):
        pltpu.make_async_copy(ref, ref, sem).wait()

    for r in range(rest):
        home = core * rest + r
        put(
            held.at[members * whole + r], shared.at[:, at_rows(blk), :],
            (home == blk) & (core == helper), where(home * teams + team, helper),
            send_sem, direct_sem.at[blk],
        )
    sent = []
    last = members - 1
    all_heads = pl.ds(0, whole)

    def send_leg(leg, kinds):
        for i in range(last):
            for g in range(whole):
                copy = pltpu.make_async_remote_copy(
                    src_ref=held.at[others[i] * whole + g, kinds],
                    dst_ref=got.at[g, kinds, at_rows(me), :],
                    send_sem=send_sem, recv_sem=recv_sem.at[leg],
                    device_id=where(others[i]), device_id_type=MESH,
                )
                copy.start()
                sent.append(copy)

    def leg_arrived(leg, kinds):
        arrived(got.at[all_heads, kinds, pl.ds(0, last * rows), :], recv_sem.at[leg])

    queries_keys, keys_values, values = pl.ds(0, 2), pl.ds(1, 2), pl.ds(2, 1)
    send_leg(0, queries_keys)
    if rest:
        @pl.when(core == helper)
        def _():
            for b in range(blks):
                arrived(shared.at[:, pl.ds(b * rows, rows), :], direct_sem.at[b])
                for turn in range(1, teams):
                    pltpu.make_async_remote_copy(
                        src_ref=shared.at[keys_values, pl.ds(b * rows, rows), :],
                        dst_ref=shared.at[keys_values, pl.ds((turn * blks + b) * rows, rows), :],
                        send_sem=send_sem, recv_sem=passed_sem,
                        device_id=where(blk * teams + lax.rem(team + turn, teams)),
                        device_id_type=MESH,
                    ).start()

    send_leg(1, values)

    for g in range(whole):
        for a in range(3):
            got[g, a, at_rows(me), :] = held[me * whole + g, a]
    leg_arrived(0, queries_keys)
    half = members // 2 * rows
    softened = [
        [soften(got[g, 0, span, :], got[g, 1]) for span in (slice(0, half), slice(half, members * rows))]
        for g in range(whole)
    ]
    passed = shared.at[keys_values, pl.ds(0, (teams - 1) * blks * rows), :]
    if rest:
        @pl.when(core == helper)
        def _():
            if teams > 1:
                arrived(passed, passed_sem)
            mine = shared[0, pl.ds(0, blks * rows), :]
            orest[...] = mix(*soften(mine, shared[1]), shared[2])
            for b in range(blks):
                put(
                    orest.at[pl.ds(b * rows, rows), :],
                    out_ref.at[:, head_cols(members * whole + blk % rest)],
                    (owner == helper) & (b == blk), where(b * teams + team, owner),
                    out_send_sem, out_sem,
                )

    leg_arrived(1, values)
    for g in range(whole):
        for start, (weights, scale) in zip((0, half), softened[g]):
            ow[g, pl.ds(start, weights.shape[0]), :] = mix(weights, scale, got[g, 2])
    for g in range(whole):
        for b in range(members):
            put(
                ow.at[g, pl.ds(b * rows, rows), :], out_ref.at[:, head_cols(me * whole + g)],
                b == me, where(b), out_send_sem, out_sem,
            )

    for copy in sent:
        copy.wait_send()
    for r in range(rest):
        @pl.when((core * rest + r != blk) | (core != helper))
        def _():
            arrived(shared.at[:, pl.ds(0, rows), :], send_sem)
    arrived(ow.at[:, pl.ds(0, last * rows), :], out_send_sem)
    if rest:
        @pl.when(core == helper)
        def _():
            if teams > 1:
                arrived(passed, send_sem)
            for b in range(blks):
                @pl.when((owner != helper) | (b != blk))
                def _():
                    arrived(orest.at[pl.ds(b * rows, rows), :], out_send_sem)
    arrived(out_ref, out_sem)


def settle_kernel(pieces, src, dst, sem):
    span = src.shape[0] // pieces
    copies = [
        pltpu.make_async_copy(
            src.at[pl.ds(i * span, span), :], dst.at[pl.ds(i * span, span), :], sem.at[i]
        )
        for i in range(pieces)
    ]
    for copy in copies:
        copy.start()
    for copy in copies:
        copy.wait()


def settled(result):
    rows = result.shape[0]
    pieces = rows // 16 if rows % 16 == 0 else 1
    return pl.pallas_call(
        partial(settle_kernel, pieces),
        out_shape=jax.ShapeDtypeStruct(result.shape, result.dtype),
        in_specs=[pl.BlockSpec(memory_space=pl.ANY)],
        out_specs=pl.BlockSpec(memory_space=pl.ANY),
        scratch_shapes=[pltpu.SemaphoreType.DMA((pieces,))],
    )(result)


def exchanged(queries, key_rows, value_rows, *, blks, teams, cores, whole, rest):
    rows, columns = queries.shape
    members = blks * teams
    bf16 = jnp.bfloat16
    return settled(pl.pallas_call(
        partial(exchange_kernel, blks, teams, cores, whole, rest),
        out_shape=jax.ShapeDtypeStruct((rows, columns), bf16),
        in_specs=[pl.BlockSpec(memory_space=pl.ANY)] * 3,
        out_specs=pl.BlockSpec(memory_space=pl.ANY),
        scratch_shapes=[
            pltpu.VMEM((3, rows, columns), bf16),
            pltpu.VMEM((columns // HD, 3, rows, HD), bf16),
            pltpu.VMEM((whole, 3, members * rows, HD), bf16),
            pltpu.VMEM((whole, members * rows, HD), bf16),
            pltpu.VMEM((3, members * rows, HD), bf16),
            pltpu.VMEM((blks * rows, HD), bf16),
            pltpu.SemaphoreType.DMA((3,)),
            pltpu.SemaphoreType.DMA,
            pltpu.SemaphoreType.DMA,
            pltpu.SemaphoreType.DMA((2,)),
            pltpu.SemaphoreType.DMA((blks,)),
            pltpu.SemaphoreType.DMA,
            pltpu.SemaphoreType.DMA,
        ],
        compiler_params=pltpu.CompilerParams(collective_id=0, has_side_effects=True),
    )(queries, key_rows, value_rows))


def solution(mesh):
    blks, teams, cores = (mesh.shape[name] for name in ("blk", "team", "head"))

    def local(queries, key_rows, value_rows):
        heads = queries.shape[1] // HD
        whole, rest = heads // (blks * teams), heads % (blks * teams)
        if whole >= 1 and blks * teams >= 2 and rest * cores in (0, blks):
            return exchanged(
                queries, key_rows, value_rows,
                blks=blks, teams=teams, cores=cores, whole=whole, rest=rest,
            )
        return gathered(queries, key_rows, value_rows)

    spec = P(("groups", "blk", "team"), "head")
    return jax.shard_map(
        local, mesh=mesh, in_specs=(spec,) * 3, out_specs=spec, check_vma=False
    )
```

```python
from functools import partial
import math

import jax
import jax.numpy as jnp
from jax import lax
from jax.experimental import pallas as pl
from jax.experimental.pallas import tpu as pltpu
from jax.sharding import PartitionSpec as P

HD = 128
MESH = pl.DeviceIdType.MESH


def attend_block(running, key_block, value_block, query_rows, score_scale):
    row_top, row_total, weighted = running
    scores = (
        jnp.einsum("qhd,khd->qhk", query_rows, key_block, preferred_element_type=jnp.float32)
        * score_scale
    )
    new_top = jnp.maximum(row_top, jnp.max(scores, axis=2))
    shrink = jnp.exp(row_top - new_top)
    weights = jnp.exp(scores - new_top[:, :, None])
    row_total = row_total * shrink + jnp.sum(weights, axis=2)
    weighted = weighted * shrink[:, :, None] + jnp.einsum(
        "qhk,khd->qhd",
        weights.astype(jnp.bfloat16),
        value_block,
        preferred_element_type=jnp.float32,
    )
    return (new_top, row_total, weighted)


def gathered(queries, key_rows, value_rows):
    own_rows = queries.shape[0]
    local_heads = queries.shape[1] // HD
    score_scale = 1.0 / math.sqrt(HD)
    query_heads = queries.reshape(own_rows, local_heads, HD)
    axes = ("blk", "team")
    keys = lax.all_gather(key_rows, axes, axis=0, tiled=True)
    values = lax.all_gather(value_rows, axes, axis=0, tiled=True)
    blocks = keys.shape[0] // own_rows
    keys = keys.reshape(blocks, own_rows, local_heads, HD)
    values = values.reshape(blocks, own_rows, local_heads, HD)

    def one_block(current, block_pair):
        return (attend_block(current, *block_pair, query_heads, score_scale), None)

    (_, row_total, weighted), _ = lax.scan(
        one_block,
        (
            jnp.full((own_rows, local_heads), -1e30, jnp.float32),
            jnp.zeros((own_rows, local_heads), jnp.float32),
            jnp.zeros((own_rows, local_heads, HD), jnp.float32),
        ),
        (keys, values),
    )
    mixed = weighted / row_total[:, :, None]
    return mixed.reshape(own_rows, local_heads * HD).astype(jnp.bfloat16)


def soften(q, k):
    scores = lax.dot_general(
        q, k, (((1,), (1,)), ((), ())), preferred_element_type=jnp.float32
    ) * (1.0 / math.sqrt(HD))
    top = jnp.max(scores, axis=1, keepdims=True)
    weights = jnp.exp(scores - top)
    return weights.astype(jnp.bfloat16), 1.0 / jnp.sum(weights, axis=1, keepdims=True)


def mix(weights, scale, v):
    mixed = jnp.dot(weights, v, preferred_element_type=jnp.float32)
    return (mixed * scale).astype(jnp.bfloat16)


def flipped(member, turn, members):
    out, bit = 0, 1
    while bit < members:
        out = out + lax.rem(member // bit + turn // bit, 2) * bit
        bit *= 2
    return out


def exchange_kernel(
    blks, teams, cores, whole, rest,
    q_ref, k_ref, v_ref, out_ref,
    staged, held, got, ow, shared, orest,
    load_sem, send_sem, out_send_sem, recv_sem, direct_sem, passed_sem, out_sem,
):
    rows = q_ref.shape[0]
    members = blks * teams
    blk, team, core = lax.axis_index("blk"), lax.axis_index("team"), lax.axis_index("head")
    me = blk * teams + team

    def where(member, on_core=core):
        return {"blk": member // teams, "team": member % teams, "head": on_core}

    def at_rows(block):
        return pl.ds(pl.multiple_of(block * rows, rows), rows)

    def head_cols(head):
        return pl.ds(pl.multiple_of(head * HD, HD), HD)

    if members & (members - 1) == 0:
        others = [flipped(me, s, members) for s in range(members - 1, 0, -1)]
    else:
        steps = sorted(range(1, members), key=lambda s: -min(s, members - s))
        others = [lax.rem(me + s, members) for s in steps]

    helper, owner = cores - 1, (blk // rest if rest else 0)

    loads = [
        pltpu.make_async_copy(src, staged.at[a], load_sem.at[a])
        for a, src in enumerate((q_ref, k_ref, v_ref))
    ]
    for load in loads:
        load.start()
    barrier = pltpu.get_barrier_semaphore()

    def greet(member, on_core):
        pl.semaphore_signal(
            barrier, inc=1, device_id=where(member, on_core), device_id_type=MESH
        )

    for other in others:
        greet(other, core)
    if rest and cores > 1:
        @pl.when(core != helper)
        def _():
            for r in range(rest):
                greet((core * rest + r) * teams + team, helper)

        @pl.when((core == helper) & (owner != helper))
        def _():
            for b in range(blks):
                greet(b * teams + team, owner)

    for a, load in enumerate(loads):
        load.wait()
        for head in range(members * whole + rest):
            held[head, a] = staged[a, :, pl.ds(head * HD, HD)]
    greeted = members - 1
    if rest and cores > 1:
        greeted = greeted + jnp.where(core != helper, rest, jnp.where(owner != helper, blks, 0))
    pl.semaphore_wait(barrier, greeted)

    def put(src, dst, here, device, sends, sem):
        @pl.when(here)
        def _():
            pltpu.make_async_copy(src, dst, sem).start()

        @pl.when(jnp.logical_not(here))
        def _():
            pltpu.make_async_remote_copy(
                src_ref=src, dst_ref=dst, send_sem=sends, recv_sem=sem,
                device_id=device, device_id_type=MESH,
            ).start()

    def arrived(ref, sem):
        pltpu.make_async_copy(ref, ref, sem).wait()

    for r in range(rest):
        home = core * rest + r
        put(
            held.at[members * whole + r], shared.at[:, at_rows(blk), :],
            (home == blk) & (core == helper), where(home * teams + team, helper),
            send_sem, direct_sem.at[blk],
        )
    sent = []
    last = members - 1
    all_heads = pl.ds(0, whole)

    def send_leg(leg, kinds):
        for i in range(last):
            for g in range(whole):
                copy = pltpu.make_async_remote_copy(
                    src_ref=held.at[others[i] * whole + g, kinds],
                    dst_ref=got.at[g, kinds, at_rows(me), :],
                    send_sem=send_sem, recv_sem=recv_sem.at[leg],
                    device_id=where(others[i]), device_id_type=MESH,
                )
                copy.start()
                sent.append(copy)

    def leg_arrived(leg, kinds):
        arrived(got.at[all_heads, kinds, pl.ds(0, last * rows), :], recv_sem.at[leg])

    queries_keys, keys_values, values = pl.ds(0, 2), pl.ds(1, 2), pl.ds(2, 1)
    send_leg(0, queries_keys)
    if rest:
        @pl.when(core == helper)
        def _():
            for b in range(blks):
                arrived(shared.at[:, pl.ds(b * rows, rows), :], direct_sem.at[b])
                for turn in range(1, teams):
                    pltpu.make_async_remote_copy(
                        src_ref=shared.at[keys_values, pl.ds(b * rows, rows), :],
                        dst_ref=shared.at[keys_values, pl.ds((turn * blks + b) * rows, rows), :],
                        send_sem=send_sem, recv_sem=passed_sem,
                        device_id=where(blk * teams + lax.rem(team + turn, teams)),
                        device_id_type=MESH,
                    ).start()

    send_leg(1, values)

    for g in range(whole):
        for a in range(3):
            got[g, a, at_rows(me), :] = held[me * whole + g, a]
    leg_arrived(0, queries_keys)
    half = members // 2 * rows
    softened = [
        [soften(got[g, 0, span, :], got[g, 1]) for span in (slice(0, half), slice(half, members * rows))]
        for g in range(whole)
    ]
    passed = shared.at[keys_values, pl.ds(0, (teams - 1) * blks * rows), :]
    if rest:
        @pl.when(core == helper)
        def _():
            if teams > 1:
                arrived(passed, passed_sem)
            mine = shared[0, pl.ds(0, blks * rows), :]
            orest[...] = mix(*soften(mine, shared[1]), shared[2])
            for b in range(blks):
                put(
                    orest.at[pl.ds(b * rows, rows), :],
                    out_ref.at[:, head_cols(members * whole + blk % rest)],
                    (owner == helper) & (b == blk), where(b * teams + team, owner),
                    out_send_sem, out_sem,
                )

    leg_arrived(1, values)
    for g in range(whole):
        for start, (weights, scale) in zip((0, half), softened[g]):
            ow[g, pl.ds(start, weights.shape[0]), :] = mix(weights, scale, got[g, 2])
    for g in range(whole):
        for b in range(members):
            put(
                ow.at[g, pl.ds(b * rows, rows), :], out_ref.at[:, head_cols(me * whole + g)],
                b == me, where(b), out_send_sem, out_sem,
            )

    for copy in sent:
        copy.wait_send()
    for r in range(rest):
        @pl.when((core * rest + r != blk) | (core != helper))
        def _():
            arrived(shared.at[:, pl.ds(0, rows), :], send_sem)
    arrived(ow.at[:, pl.ds(0, last * rows), :], out_send_sem)
    if rest:
        @pl.when(core == helper)
        def _():
            if teams > 1:
                arrived(passed, send_sem)
            for b in range(blks):
                @pl.when((owner != helper) | (b != blk))
                def _():
                    arrived(orest.at[pl.ds(b * rows, rows), :], out_send_sem)
    arrived(out_ref, out_sem)


def exchanged(queries, key_rows, value_rows, *, blks, teams, cores, whole, rest):
    rows, columns = queries.shape
    members = blks * teams
    bf16 = jnp.bfloat16
    return pl.pallas_call(
        partial(exchange_kernel, blks, teams, cores, whole, rest),
        out_shape=jax.ShapeDtypeStruct((rows, columns), bf16),
        in_specs=[pl.BlockSpec(memory_space=pl.ANY)] * 3,
        out_specs=pl.BlockSpec(memory_space=pl.ANY),
        scratch_shapes=[
            pltpu.VMEM((3, rows, columns), bf16),
            pltpu.VMEM((columns // HD, 3, rows, HD), bf16),
            pltpu.VMEM((whole, 3, members * rows, HD), bf16),
            pltpu.VMEM((whole, members * rows, HD), bf16),
            pltpu.VMEM((3, members * rows, HD), bf16),
            pltpu.VMEM((blks * rows, HD), bf16),
            pltpu.SemaphoreType.DMA((3,)),
            pltpu.SemaphoreType.DMA,
            pltpu.SemaphoreType.DMA,
            pltpu.SemaphoreType.DMA((2,)),
            pltpu.SemaphoreType.DMA((blks,)),
            pltpu.SemaphoreType.DMA,
            pltpu.SemaphoreType.DMA,
        ],
        compiler_params=pltpu.CompilerParams(
            collective_id=0, has_side_effects=True, vmem_limit_bytes=16 * 3 * queries.size * queries.dtype.itemsize
        ),
    )(queries, key_rows, value_rows)


def solution(mesh):
    blks, teams, cores = (mesh.shape[name] for name in ("blk", "team", "head"))

    def local(queries, key_rows, value_rows):
        heads = queries.shape[1] // HD
        whole, rest = heads // (blks * teams), heads % (blks * teams)
        if whole >= 1 and blks * teams >= 2 and rest * cores in (0, blks):
            return exchanged(
                queries, key_rows, value_rows,
                blks=blks, teams=teams, cores=cores, whole=whole, rest=rest,
            )
        return gathered(queries, key_rows, value_rows)

    spec = P(("groups", "blk", "team"), "head")
    return jax.shard_map(
        local, mesh=mesh, in_specs=(spec,) * 3, out_specs=spec, check_vma=False
    )
```

```python
from functools import partial
import math

import jax
import jax.numpy as jnp
from jax import lax
from jax.experimental import pallas as pl
from jax.experimental.pallas import tpu as pltpu
from jax.sharding import PartitionSpec as P

HD = 128
MESH = pl.DeviceIdType.MESH


def attend_block(running, key_block, value_block, query_rows, score_scale):
    row_top, row_total, weighted = running
    scores = (
        jnp.einsum("qhd,khd->qhk", query_rows, key_block, preferred_element_type=jnp.float32)
        * score_scale
    )
    new_top = jnp.maximum(row_top, jnp.max(scores, axis=2))
    shrink = jnp.exp(row_top - new_top)
    weights = jnp.exp(scores - new_top[:, :, None])
    row_total = row_total * shrink + jnp.sum(weights, axis=2)
    weighted = weighted * shrink[:, :, None] + jnp.einsum(
        "qhk,khd->qhd",
        weights.astype(jnp.bfloat16),
        value_block,
        preferred_element_type=jnp.float32,
    )
    return (new_top, row_total, weighted)


def gathered(queries, key_rows, value_rows):
    own_rows = queries.shape[0]
    local_heads = queries.shape[1] // HD
    score_scale = 1.0 / math.sqrt(HD)
    query_heads = queries.reshape(own_rows, local_heads, HD)
    axes = ("blk", "team")
    keys = lax.all_gather(key_rows, axes, axis=0, tiled=True)
    values = lax.all_gather(value_rows, axes, axis=0, tiled=True)
    blocks = keys.shape[0] // own_rows
    keys = keys.reshape(blocks, own_rows, local_heads, HD)
    values = values.reshape(blocks, own_rows, local_heads, HD)

    def one_block(current, block_pair):
        return (attend_block(current, *block_pair, query_heads, score_scale), None)

    (_, row_total, weighted), _ = lax.scan(
        one_block,
        (
            jnp.full((own_rows, local_heads), -1e30, jnp.float32),
            jnp.zeros((own_rows, local_heads), jnp.float32),
            jnp.zeros((own_rows, local_heads, HD), jnp.float32),
        ),
        (keys, values),
    )
    mixed = weighted / row_total[:, :, None]
    return mixed.reshape(own_rows, local_heads * HD).astype(jnp.bfloat16)


def soften(q, k):
    scores = lax.dot_general(
        q, k, (((1,), (1,)), ((), ())), preferred_element_type=jnp.float32
    ) * (1.0 / math.sqrt(HD))
    top = jnp.max(scores, axis=1, keepdims=True)
    weights = jnp.exp(scores - top)
    return weights.astype(jnp.bfloat16), 1.0 / jnp.sum(weights, axis=1, keepdims=True)


def mix(weights, scale, v):
    mixed = jnp.dot(weights, v, preferred_element_type=jnp.float32)
    return (mixed * scale).astype(jnp.bfloat16)


def flipped(member, turn, members):
    out, bit = 0, 1
    while bit < members:
        out = out + lax.rem(member // bit + turn // bit, 2) * bit
        bit *= 2
    return out


def exchange_kernel(
    blks, teams, cores, whole, rest,
    q_ref, k_ref, v_ref, out_ref,
    staged, held, got, ow, shared, orest,
    load_sem, send_sem, out_send_sem, recv_sem, direct_sem, passed_sem, out_sem,
):
    rows = q_ref.shape[0]
    members = blks * teams
    blk, team, core = lax.axis_index("blk"), lax.axis_index("team"), lax.axis_index("head")
    me = blk * teams + team

    def where(member, on_core=core):
        return {"blk": member // teams, "team": member % teams, "head": on_core}

    def at_rows(block):
        return pl.ds(pl.multiple_of(block * rows, rows), rows)

    def head_cols(head):
        return pl.ds(pl.multiple_of(head * HD, HD), HD)

    if members & (members - 1) == 0:
        others = [flipped(me, s, members) for s in range(members - 1, 0, -1)]
    else:
        steps = sorted(range(1, members), key=lambda s: -min(s, members - s))
        others = [lax.rem(me + s, members) for s in steps]

    helper, owner = cores - 1, (blk // rest if rest else 0)

    loads = [
        pltpu.make_async_copy(src, staged.at[a], load_sem.at[a])
        for a, src in enumerate((q_ref, k_ref, v_ref))
    ]
    for load in loads:
        load.start()
    barrier = pltpu.get_barrier_semaphore()

    def greet(member, on_core):
        pl.semaphore_signal(
            barrier, inc=1, device_id=where(member, on_core), device_id_type=MESH
        )

    for other in others:
        greet(other, core)
    if rest and cores > 1:
        @pl.when(core != helper)
        def _():
            for r in range(rest):
                greet((core * rest + r) * teams + team, helper)

        @pl.when((core == helper) & (owner != helper))
        def _():
            for b in range(blks):
                greet(b * teams + team, owner)

    for a, load in enumerate(loads):
        load.wait()
        for head in range(members * whole + rest):
            held[head, a] = staged[a, :, pl.ds(head * HD, HD)]
    greeted = members - 1
    if rest and cores > 1:
        greeted = greeted + jnp.where(core != helper, rest, jnp.where(owner != helper, blks, 0))
    pl.semaphore_wait(barrier, greeted)

    def put(src, dst, here, device, sends, sem):
        @pl.when(here)
        def _():
            pltpu.make_async_copy(src, dst, sem).start()

        @pl.when(jnp.logical_not(here))
        def _():
            pltpu.make_async_remote_copy(
                src_ref=src, dst_ref=dst, send_sem=sends, recv_sem=sem,
                device_id=device, device_id_type=MESH,
            ).start()

    def arrived(ref, sem):
        pltpu.make_async_copy(ref, ref, sem).wait()

    for r in range(rest):
        home = core * rest + r
        put(
            held.at[members * whole + r], shared.at[:, at_rows(blk), :],
            (home == blk) & (core == helper), where(home * teams + team, helper),
            send_sem, direct_sem.at[blk],
        )
    sent = []
    last = members - 1
    all_heads = pl.ds(0, whole)

    def send_leg(leg, kinds):
        for i in range(last):
            for g in range(whole):
                copy = pltpu.make_async_remote_copy(
                    src_ref=held.at[others[i] * whole + g, kinds],
                    dst_ref=got.at[g, kinds, at_rows(me), :],
                    send_sem=send_sem, recv_sem=recv_sem.at[leg],
                    device_id=where(others[i]), device_id_type=MESH,
                )
                copy.start()
                sent.append(copy)

    def leg_arrived(leg, kinds):
        arrived(got.at[all_heads, kinds, pl.ds(0, last * rows), :], recv_sem.at[leg])

    queries_keys, keys_values, values = pl.ds(0, 2), pl.ds(1, 2), pl.ds(2, 1)
    send_leg(0, queries_keys)
    if rest:
        @pl.when(core == helper)
        def _():
            for b in range(blks):
                arrived(shared.at[:, pl.ds(b * rows, rows), :], direct_sem.at[b])
                for turn in range(1, teams):
                    pltpu.make_async_remote_copy(
                        src_ref=shared.at[keys_values, pl.ds(b * rows, rows), :],
                        dst_ref=shared.at[keys_values, pl.ds((turn * blks + b) * rows, rows), :],
                        send_sem=send_sem, recv_sem=passed_sem,
                        device_id=where(blk * teams + lax.rem(team + turn, teams)),
                        device_id_type=MESH,
                    ).start()

    send_leg(1, values)

    for g in range(whole):
        for a in range(3):
            got[g, a, at_rows(me), :] = held[me * whole + g, a]
    leg_arrived(0, queries_keys)
    half = members // 2 * rows
    softened = [
        [soften(got[g, 0, span, :], got[g, 1]) for span in (slice(0, half), slice(half, members * rows))]
        for g in range(whole)
    ]
    passed = shared.at[keys_values, pl.ds(0, (teams - 1) * blks * rows), :]
    if rest:
        @pl.when(core == helper)
        def _():
            if teams > 1:
                arrived(passed, passed_sem)
            mine = shared[0, pl.ds(0, blks * rows), :]
            orest[...] = mix(*soften(mine, shared[1]), shared[2])
            for b in range(blks):
                put(
                    orest.at[pl.ds(b * rows, rows), :],
                    out_ref.at[:, head_cols(members * whole + blk % rest)],
                    (owner == helper) & (b == blk), where(b * teams + team, owner),
                    out_send_sem, out_sem,
                )

    leg_arrived(1, values)
    for g in range(whole):
        for start, (weights, scale) in zip((0, half), softened[g]):
            ow[g, pl.ds(start, weights.shape[0]), :] = mix(weights, scale, got[g, 2])
    for g in range(whole):
        for b in range(members):
            put(
                ow.at[g, pl.ds(b * rows, rows), :], out_ref.at[:, head_cols(me * whole + g)],
                b == me, where(b), out_send_sem, out_sem,
            )

    for copy in sent:
        copy.wait_send()
    for r in range(rest):
        @pl.when((core * rest + r != blk) | (core != helper))
        def _():
            arrived(shared.at[:, pl.ds(0, rows), :], send_sem)
    arrived(ow.at[:, pl.ds(0, last * rows), :], out_send_sem)
    if rest:
        @pl.when(core == helper)
        def _():
            if teams > 1:
                arrived(passed, send_sem)
            for b in range(blks):
                @pl.when((owner != helper) | (b != blk))
                def _():
                    arrived(orest.at[pl.ds(b * rows, rows), :], out_send_sem)
    arrived(out_ref, out_sem)


def exchanged(queries, key_rows, value_rows, *, blks, teams, cores, whole, rest):
    rows, columns = queries.shape
    members = blks * teams
    bf16 = jnp.bfloat16
    return pl.pallas_call(
        partial(exchange_kernel, blks, teams, cores, whole, rest),
        out_shape=pltpu.VMEM((rows, columns), bf16),
        in_specs=[pl.BlockSpec(memory_space=pl.ANY)] * 3,
        out_specs=pl.BlockSpec(memory_space=pl.ANY),
        scratch_shapes=[
            pltpu.VMEM((3, rows, columns), bf16),
            pltpu.VMEM((columns // HD, 3, rows, HD), bf16),
            pltpu.VMEM((whole, 3, members * rows, HD), bf16),
            pltpu.VMEM((whole, members * rows, HD), bf16),
            pltpu.VMEM((3, members * rows, HD), bf16),
            pltpu.VMEM((blks * rows, HD), bf16),
            pltpu.SemaphoreType.DMA((3,)),
            pltpu.SemaphoreType.DMA,
            pltpu.SemaphoreType.DMA,
            pltpu.SemaphoreType.DMA((2,)),
            pltpu.SemaphoreType.DMA((blks,)),
            pltpu.SemaphoreType.DMA,
            pltpu.SemaphoreType.DMA,
        ],
        compiler_params=pltpu.CompilerParams(
            collective_id=0, has_side_effects=True, vmem_limit_bytes=16 * 3 * queries.size * queries.dtype.itemsize
        ),
    )(*(pltpu.with_memory_space_constraint(x, pltpu.HBM) for x in (queries, key_rows, value_rows)))


def solution(mesh):
    blks, teams, cores = (mesh.shape[name] for name in ("blk", "team", "head"))

    def local(queries, key_rows, value_rows):
        heads = queries.shape[1] // HD
        whole, rest = heads // (blks * teams), heads % (blks * teams)
        if whole >= 1 and blks * teams >= 2 and rest * cores in (0, blks):
            return exchanged(
                queries, key_rows, value_rows,
                blks=blks, teams=teams, cores=cores, whole=whole, rest=rest,
            )
        return gathered(queries, key_rows, value_rows)

    spec = P(("groups", "blk", "team"), "head")
    return jax.shard_map(
        local, mesh=mesh, in_specs=(spec,) * 3, out_specs=spec, check_vma=False
    )
```

```python
from functools import partial
import math

import jax
import jax.numpy as jnp
from jax import lax
from jax.experimental import pallas as pl
from jax.experimental.pallas import tpu as pltpu
from jax.sharding import PartitionSpec as P

HD = 128
MESH = pl.DeviceIdType.MESH


def attend_block(running, key_block, value_block, query_rows, score_scale):
    row_top, row_total, weighted = running
    scores = (
        jnp.einsum("qhd,khd->qhk", query_rows, key_block, preferred_element_type=jnp.float32)
        * score_scale
    )
    new_top = jnp.maximum(row_top, jnp.max(scores, axis=2))
    shrink = jnp.exp(row_top - new_top)
    weights = jnp.exp(scores - new_top[:, :, None])
    row_total = row_total * shrink + jnp.sum(weights, axis=2)
    weighted = weighted * shrink[:, :, None] + jnp.einsum(
        "qhk,khd->qhd",
        weights.astype(jnp.bfloat16),
        value_block,
        preferred_element_type=jnp.float32,
    )
    return (new_top, row_total, weighted)


def gathered(queries, key_rows, value_rows):
    own_rows = queries.shape[0]
    local_heads = queries.shape[1] // HD
    score_scale = 1.0 / math.sqrt(HD)
    query_heads = queries.reshape(own_rows, local_heads, HD)
    axes = ("blk", "team")
    keys = lax.all_gather(key_rows, axes, axis=0, tiled=True)
    values = lax.all_gather(value_rows, axes, axis=0, tiled=True)
    blocks = keys.shape[0] // own_rows
    keys = keys.reshape(blocks, own_rows, local_heads, HD)
    values = values.reshape(blocks, own_rows, local_heads, HD)

    def one_block(current, block_pair):
        return (attend_block(current, *block_pair, query_heads, score_scale), None)

    (_, row_total, weighted), _ = lax.scan(
        one_block,
        (
            jnp.full((own_rows, local_heads), -1e30, jnp.float32),
            jnp.zeros((own_rows, local_heads), jnp.float32),
            jnp.zeros((own_rows, local_heads, HD), jnp.float32),
        ),
        (keys, values),
    )
    mixed = weighted / row_total[:, :, None]
    return mixed.reshape(own_rows, local_heads * HD).astype(jnp.bfloat16)


def soften(q, k):
    scores = lax.dot_general(
        q, k, (((1,), (1,)), ((), ())), preferred_element_type=jnp.float32
    ) * (1.0 / math.sqrt(HD))
    top = jnp.max(scores, axis=1, keepdims=True)
    weights = jnp.exp(scores - top)
    return weights.astype(jnp.bfloat16), 1.0 / jnp.sum(weights, axis=1, keepdims=True)


def mix(weights, scale, v):
    mixed = jnp.dot(weights, v, preferred_element_type=jnp.float32)
    return (mixed * scale).astype(jnp.bfloat16)


def flipped(member, turn, members):
    out, bit = 0, 1
    while bit < members:
        out = out + lax.rem(member // bit + turn // bit, 2) * bit
        bit *= 2
    return out


def exchange_kernel(
    blks, teams, cores, whole, rest,
    q_ref, k_ref, v_ref, out_ref,
    staged, held, got, ow, shared, orest,
    load_sem, send_sem, out_send_sem, recv_sem, direct_sem, passed_sem, out_sem,
):
    rows = q_ref.shape[0]
    members = blks * teams
    blk, team, core = lax.axis_index("blk"), lax.axis_index("team"), lax.axis_index("head")
    me = blk * teams + team

    def where(member, on_core=core):
        return {"blk": member // teams, "team": member % teams, "head": on_core}

    def at_rows(block):
        return pl.ds(pl.multiple_of(block * rows, rows), rows)

    def head_cols(head):
        return pl.ds(pl.multiple_of(head * HD, HD), HD)

    if members & (members - 1) == 0:
        others = [flipped(me, s, members) for s in range(members - 1, 0, -1)]
    else:
        steps = sorted(range(1, members), key=lambda s: -min(s, members - s))
        others = [lax.rem(me + s, members) for s in steps]

    helper, owner = cores - 1, (blk // rest if rest else 0)

    loads = [
        pltpu.make_async_copy(src, staged.at[a], load_sem.at[a])
        for a, src in enumerate((q_ref, k_ref, v_ref))
    ]
    for load in loads:
        load.start()
    barrier = pltpu.get_barrier_semaphore()

    def greet(member, on_core):
        pl.semaphore_signal(
            barrier, inc=1, device_id=where(member, on_core), device_id_type=MESH
        )

    for other in others:
        greet(other, core)
    if rest and cores > 1:
        @pl.when(core != helper)
        def _():
            for r in range(rest):
                greet((core * rest + r) * teams + team, helper)

        @pl.when((core == helper) & (owner != helper))
        def _():
            for b in range(blks):
                greet(b * teams + team, owner)

    for a, load in enumerate(loads):
        load.wait()
        for head in range(members * whole + rest):
            held[head, a] = staged[a, :, pl.ds(head * HD, HD)]
    greeted = members - 1
    if rest and cores > 1:
        greeted = greeted + jnp.where(core != helper, rest, jnp.where(owner != helper, blks, 0))
    pl.semaphore_wait(barrier, greeted)

    def put(src, dst, here, device, sends, sem):
        @pl.when(here)
        def _():
            pltpu.make_async_copy(src, dst, sem).start()

        @pl.when(jnp.logical_not(here))
        def _():
            pltpu.make_async_remote_copy(
                src_ref=src, dst_ref=dst, send_sem=sends, recv_sem=sem,
                device_id=device, device_id_type=MESH,
            ).start()

    def arrived(ref, sem):
        pltpu.make_async_copy(ref, ref, sem).wait()

    for r in range(rest):
        home = core * rest + r
        put(
            held.at[members * whole + r], shared.at[:, at_rows(blk), :],
            (home == blk) & (core == helper), where(home * teams + team, helper),
            send_sem, direct_sem.at[blk],
        )
    sent = []
    last = members - 1
    all_heads = pl.ds(0, whole)

    def send_leg(leg, kinds):
        for i in range(last):
            for g in range(whole):
                copy = pltpu.make_async_remote_copy(
                    src_ref=held.at[others[i] * whole + g, kinds],
                    dst_ref=got.at[g, kinds, at_rows(me), :],
                    send_sem=send_sem, recv_sem=recv_sem.at[leg],
                    device_id=where(others[i]), device_id_type=MESH,
                )
                copy.start()
                sent.append(copy)

    def leg_arrived(leg, kinds):
        arrived(got.at[all_heads, kinds, pl.ds(0, last * rows), :], recv_sem.at[leg])

    queries_keys, keys_values, values = pl.ds(0, 2), pl.ds(1, 2), pl.ds(2, 1)
    send_leg(0, queries_keys)
    if rest:
        @pl.when(core == helper)
        def _():
            for b in range(blks):
                arrived(shared.at[:, pl.ds(b * rows, rows), :], direct_sem.at[b])
                for turn in range(1, teams):
                    pltpu.make_async_remote_copy(
                        src_ref=shared.at[keys_values, pl.ds(b * rows, rows), :],
                        dst_ref=shared.at[keys_values, pl.ds((turn * blks + b) * rows, rows), :],
                        send_sem=send_sem, recv_sem=passed_sem,
                        device_id=where(blk * teams + lax.rem(team + turn, teams)),
                        device_id_type=MESH,
                    ).start()

    send_leg(1, values)

    for g in range(whole):
        for a in range(3):
            got[g, a, at_rows(me), :] = held[me * whole + g, a]
    leg_arrived(0, queries_keys)
    half = members // 2 * rows
    softened = [
        [soften(got[g, 0, span, :], got[g, 1]) for span in (slice(0, half), slice(half, members * rows))]
        for g in range(whole)
    ]
    passed = shared.at[keys_values, pl.ds(0, (teams - 1) * blks * rows), :]
    if rest:
        @pl.when(core == helper)
        def _():
            if teams > 1:
                arrived(passed, passed_sem)
            mine = shared[0, pl.ds(0, blks * rows), :]
            orest[...] = mix(*soften(mine, shared[1]), shared[2])
            for b in range(blks):
                put(
                    orest.at[pl.ds(b * rows, rows), :],
                    out_ref.at[:, head_cols(members * whole + blk % rest)],
                    (owner == helper) & (b == blk), where(b * teams + team, owner),
                    out_send_sem, out_sem,
                )

    leg_arrived(1, values)
    for g in range(whole):
        for start, (weights, scale) in zip((0, half), softened[g]):
            ow[g, pl.ds(start, weights.shape[0]), :] = mix(weights, scale, got[g, 2])
            for b in range(start // rows, (start + weights.shape[0]) // rows):
                put(
                    ow.at[g, pl.ds(b * rows, rows), :],
                    out_ref.at[:, head_cols(me * whole + g)],
                    b == me, where(b), out_send_sem, out_sem,
                )

    for copy in sent:
        copy.wait_send()
    for r in range(rest):
        @pl.when((core * rest + r != blk) | (core != helper))
        def _():
            arrived(shared.at[:, pl.ds(0, rows), :], send_sem)
    arrived(ow.at[:, pl.ds(0, last * rows), :], out_send_sem)
    if rest:
        @pl.when(core == helper)
        def _():
            if teams > 1:
                arrived(passed, send_sem)
            for b in range(blks):
                @pl.when((owner != helper) | (b != blk))
                def _():
                    arrived(orest.at[pl.ds(b * rows, rows), :], out_send_sem)
    arrived(out_ref, out_sem)


def exchanged(queries, key_rows, value_rows, *, blks, teams, cores, whole, rest):
    rows, columns = queries.shape
    members = blks * teams
    bf16 = jnp.bfloat16
    return pl.pallas_call(
        partial(exchange_kernel, blks, teams, cores, whole, rest),
        out_shape=pltpu.VMEM((rows, columns), bf16),
        in_specs=[pl.BlockSpec(memory_space=pl.ANY)] * 3,
        out_specs=pl.BlockSpec(memory_space=pl.ANY),
        scratch_shapes=[
            pltpu.VMEM((3, rows, columns), bf16),
            pltpu.VMEM((columns // HD, 3, rows, HD), bf16),
            pltpu.VMEM((whole, 3, members * rows, HD), bf16),
            pltpu.VMEM((whole, members * rows, HD), bf16),
            pltpu.VMEM((3, members * rows, HD), bf16),
            pltpu.VMEM((blks * rows, HD), bf16),
            pltpu.SemaphoreType.DMA((3,)),
            pltpu.SemaphoreType.DMA,
            pltpu.SemaphoreType.DMA,
            pltpu.SemaphoreType.DMA((2,)),
            pltpu.SemaphoreType.DMA((blks,)),
            pltpu.SemaphoreType.DMA,
            pltpu.SemaphoreType.DMA,
        ],
        compiler_params=pltpu.CompilerParams(
            collective_id=0, has_side_effects=True, vmem_limit_bytes=16 * 3 * queries.size * queries.dtype.itemsize
        ),
    )(*(pltpu.with_memory_space_constraint(x, pltpu.HBM) for x in (queries, key_rows, value_rows)))


def solution(mesh):
    blks, teams, cores = (mesh.shape[name] for name in ("blk", "team", "head"))

    def local(queries, key_rows, value_rows):
        heads = queries.shape[1] // HD
        whole, rest = heads // (blks * teams), heads % (blks * teams)
        if whole >= 1 and blks * teams >= 2 and rest * cores in (0, blks):
            return exchanged(
                queries, key_rows, value_rows,
                blks=blks, teams=teams, cores=cores, whole=whole, rest=rest,
            )
        return gathered(queries, key_rows, value_rows)

    spec = P(("groups", "blk", "team"), "head")
    return jax.shard_map(
        local, mesh=mesh, in_specs=(spec,) * 3, out_specs=spec, check_vma=False
    )
```
